256 devices in a mesh: width: 8 (over x, core), latent: 32 (over z, y).
Axes of the slice: x: 4, y: 4, z: 8, core: 2. Of those that a mesh axis runs over, the one named last changes fastest.
Arguments:
- activations: bfloat16 [256, 4608], P(None, 'width'), may hold values from -6 to 6
- encoder: bfloat16 [4608, 65536], P('width', 'latent'), may hold values from -0.09375 to 0.09375
- latent_bias: float32 [65536], P('latent'), may hold values from -0.6 to 0.2
- decoder: bfloat16 [65536, 4608], P('latent', 'width')
- output_bias: float32 [4608], P('width'), may hold values from -3 to 3
Outputs:
- loss_value: float32 [], replicated
- encoder_grad: bfloat16 [4608, 65536], P('width', 'latent')
- latent_grad: float32 [65536], P('latent')
- decoder_grad: bfloat16 [65536, 4608], P('latent', 'width')
- output_grad: float32 [4608], P('width')
The draws below stay inside these ranges and needn't reach their ends.
All inputs are finite; a program needn't handle non-finite values.
Results may differ from the reference program's by a relative error of at most 0.018.
Values may be sent and summed in bfloat16 or wider, within the bound.
No kernel may reach another device: no remote copies, remote signals or barrier semaphores. Data moves between devices by JAX's collectives and lax.ppermute only.
A program may use at most 64 MiB of HBM per device.

```python
import math
import jax
import jax.numpy as jnp
from jax import lax

D = 2304
LAYERS = 2
F = 65536
TOK = 256
LD = 4608


def draw_decoder(key, part):
    key = jax.random.fold_in(key, 7)
    key_entries, key_rows, key_columns, key_signs = jax.random.split(key, 4)
    positions = jnp.arange(LAYERS * D, dtype=jnp.float32) / (LAYERS * D - 1)
    block_count = LAYERS * D // 64
    block_scale = jnp.exp(jax.random.uniform(key_rows, (F, block_count), dtype=jnp.float32) * math.log(10.0))
    row_scale = jnp.repeat(block_scale, 64, axis=1)
    signs = (jax.random.randint(key_signs, (LAYERS * D,), 0, 2) * 2 - 1).astype(jnp.float32)
    entries = jnp.clip(jax.random.normal(key_entries, (F, LAYERS * D), dtype=jnp.float32), -4.0, 4.0)
    rising = math.log(3.0)
    common = 0.025
    jitter = jax.random.uniform(key_columns, (LAYERS * D,), dtype=jnp.float32) * math.log(10.0 / 3.0)
    column_scale = jnp.exp(rising * positions + jitter)
    mixed = entries + common * signs[None, :]
    return (mixed * row_scale * column_scale[None, :] / (14.0 * math.sqrt(F))).astype(jnp.bfloat16)


def level_of(own_key, dims, cuts, low, largest):
    def one(dim, shards_of):
        steps = jax.random.uniform(jax.random.fold_in(jax.random.fold_in(own_key, 6), dim), (shards_of,), jnp.float32, low / len(cuts), largest / len(cuts))
        return jnp.repeat(jnp.exp(steps), dims[dim] // shards_of).reshape((-1,) + (1,) * (len(dims) - dim - 1))

    level = one(*cuts[0])
    for cut in cuts[1:]:
        level = level * one(*cut)
    return level


def bell_draw(rng, dims, deviation, most, pieces=(), kind=jnp.bfloat16):
    loudness = level_of(rng, dims, pieces, -0.22, 0.18) if pieces else 1.0
    values = jax.random.normal(rng, dims, jnp.float32) * deviation * loudness
    return jnp.minimum(jnp.maximum(values, -most), most).astype(kind)


def setup_inputs(seed: int = 0) -> dict:
    arg_keys = jax.random.split(jax.random.key(seed), 6)
    activations = bell_draw(arg_keys[0], (TOK, LD), 1.0, 6.0, ((1, 8),))
    encoder = bell_draw(arg_keys[1], (LD, F), LD ** -0.5, 0.09375, ((0, 8), (1, 32)))
    latent_bias = jnp.clip(-0.6 + 0.8 * jax.random.uniform(arg_keys[2], (F,), jnp.float32) ** level_of(arg_keys[2], (F,), ((0, 32),), -0.2, 0.2), -0.6, 0.2)
    decoder = draw_decoder(jax.random.fold_in(arg_keys[5], 71), 0)
    output_bias = bell_draw(arg_keys[4], (LD,), 0.5, 3.0, ((0, 8),), jnp.float32)
    return {"activations": activations, "encoder": encoder, "latent_bias": latent_bias, "decoder": decoder, "output_bias": output_bias}


SPARSITY = 0.5
EPSILON = 1e-06

def reference(activations, encoder, latent_bias, decoder, output_bias):
    preact = jnp.dot(activations, encoder, preferred_element_type=jnp.float32) + latent_bias
    features = jnp.maximum(preact, 0.0).astype(jnp.bfloat16)
    rebuilt = jnp.dot(features, decoder, preferred_element_type=jnp.float32) + output_bias
    errors = rebuilt - activations.astype(jnp.float32)
    block_size = math.gcd(F, 4096)
    block_count = F // block_size
    blocks = decoder.reshape(block_count, block_size, LAYERS, D)

    def block_norms(piece):
        return jnp.sqrt(lax.optimization_barrier(jnp.sum(jnp.square(piece.astype(jnp.float32)), axis=-1)) + EPSILON)
    norms = lax.map(block_norms, blocks).reshape(F, LAYERS)
    weights = lax.optimization_barrier(jnp.sum(norms, axis=1))
    feature_totals = lax.optimization_barrier(jnp.sum(features.astype(jnp.float32), axis=0))
    loss_value = (0.5 * jnp.sum(errors * errors) + SPARSITY * jnp.sum(feature_totals * weights)) / (TOK * LAYERS * D)
    error_half = errors.astype(jnp.bfloat16)
    output_grad = lax.optimization_barrier(jnp.sum(error_half.astype(jnp.float32), axis=0))
    grad_feat = jnp.dot(error_half, decoder.T, preferred_element_type=jnp.float32) + SPARSITY * weights
    grad_pre = jnp.where(features > 0, grad_feat, 0.0).astype(jnp.bfloat16)
    encoder_grad = jnp.dot(activations.T, grad_pre, preferred_element_type=jnp.float32).astype(jnp.bfloat16)
    latent_grad = lax.optimization_barrier(jnp.sum(grad_pre.astype(jnp.float32), axis=0))
    feature_blocks = features.reshape(TOK, block_count, block_size).transpose(1, 0, 2)
    norm_blocks = norms.reshape(block_count, block_size, LAYERS)
    total_blocks = feature_totals.reshape(block_count, block_size)

    def decoder_block(inputs):
        feat_piece, weight_piece, norm_piece, total_piece = inputs
        direct = jnp.dot(feat_piece.T, error_half, preferred_element_type=jnp.float32).reshape(block_size, LAYERS, D)
        shrink = SPARSITY * total_piece[:, None, None] * weight_piece.astype(jnp.float32) / norm_piece[:, :, None]
        return (direct + shrink).astype(jnp.bfloat16).reshape(block_size, LAYERS * D)
    decoder_grad = lax.map(decoder_block, (feature_blocks, blocks, norm_blocks, total_blocks)).reshape(F, LAYERS * D)
    return (loss_value, encoder_grad, latent_grad, decoder_grad, output_grad)
```

```python
import jax
import jax.numpy as jnp
from jax import lax
from jax.experimental import pallas as pl
from jax.experimental.pallas import tpu as pltpu
from jax.sharding import PartitionSpec as P

D = 2304
LAYERS = 2
SPARSITY = 0.5
EPSILON = 1e-06
F32 = jnp.float32
BF16 = jnp.bfloat16
TOK = 256
COL = 576
CHUNK = 256
WIDE = 640
LAT = 2048
VMEM_BYTES = 20 * 1024 * 1024

CORE_SWAP = [(i, i ^ 1) for i in range(8)]
X_PAIR_NEAR = [(i, ((i // 2) ^ 1) * 2 + i % 2) for i in range(8)]
X_PAIR_FAR = [(i, (3 - i // 2) * 2 + i % 2) for i in range(8)]


def x_shift(d):
    return [(i, (i + 2 * d) % 8) for i in range(8)]


def on_width(value, pairs):
    return lax.ppermute(value, "width", pairs)


def dot(a, b, dims):
    return lax.dot_general(a, b, (dims, ((), ())), preferred_element_type=F32)


def params():
    return pltpu.CompilerParams(vmem_limit_bytes=VMEM_BYTES)


def whole(shape):
    return pl.BlockSpec(shape, lambda *_: (0,) * len(shape))


def four_chunks(left, matrix, order, contract, kind, name):
    rows = matrix.shape[0]

    def body(order_ref, left_ref, matrix_ref, *outs):
        step = pl.program_id(0)
        if contract == 0:
            value = dot(left_ref[...], matrix_ref[...], ((0,), (0,)))
        else:
            value = dot(left_ref[:, :COL], matrix_ref[...], ((1,), (0,)))
        for k in range(4):
            @pl.when(step == k)
            def _():
                outs[k][...] = value.astype(kind)

    return pl.pallas_call(
        body,
        grid_spec=pltpu.PrefetchScalarGridSpec(
            num_scalar_prefetch=1,
            grid=(4,),
            in_specs=[whole(left.shape), pl.BlockSpec((rows, CHUNK), lambda i, order: (0, order[i]))],
            out_specs=[whole((TOK, CHUNK))] * 4,
        ),
        out_shape=[jax.ShapeDtypeStruct((TOK, CHUNK), kind)] * 4,
        compiler_params=params(),
        name=name,
        cost_estimate=pl.CostEstimate(
            flops=2 * TOK * COL * CHUNK * 4, bytes_accessed=COL * CHUNK * 8 + TOK * CHUNK * 16, transcendentals=0
        ),
    )(order, left, matrix)


def rebuild(chunks, order, dec_t, own_weights):
    def body(order_ref, *refs):
        feats, (dec_ref, weight_ref, out_ref, acc, extra) = refs[:8], refs[8:]
        step = pl.program_id(0)
        for k in range(8):
            @pl.when(step == k)
            def _():
                value = dot(feats[k][...], dec_ref[...], ((1,), (1,)))
                if k == 0:
                    acc[...] = value
                    extra[...] = jnp.sum(feats[0][...].astype(F32) * weight_ref[...], axis=1, keepdims=True)
                else:
                    acc[...] += value

        @pl.when(step == 7)
        def _():
            out_ref[:, :COL] = acc[...].astype(BF16)
            out_ref[:, COL:] = jnp.broadcast_to(extra[...], (TOK, WIDE - COL)).astype(BF16)

    return pl.pallas_call(
        body,
        grid_spec=pltpu.PrefetchScalarGridSpec(
            num_scalar_prefetch=1,
            grid=(8,),
            in_specs=[whole((TOK, CHUNK))] * 8
            + [pl.BlockSpec((COL, CHUNK), lambda i, order: (0, order[i])), whole((1, CHUNK))],
            out_specs=whole((TOK, WIDE)),
            scratch_shapes=[pltpu.VMEM((TOK, COL), F32), pltpu.VMEM((TOK, 1), F32)],
        ),
        out_shape=jax.ShapeDtypeStruct((TOK, WIDE), BF16),
        compiler_params=params(),
        name="rebuild",
        cost_estimate=pl.CostEstimate(
            flops=2 * TOK * COL * LAT, bytes_accessed=COL * LAT * 2 + TOK * LAT * 2, transcendentals=0
        ),
    )(order, *chunks, dec_t, own_weights)


def error_rows(parts, offset):
    def body(parts_ref, offset_ref, out_ref):
        total = jnp.sum(parts_ref[...].astype(F32), axis=0)
        errors = total[:, :COL] + offset_ref[...]
        loss = 0.5 * jnp.sum(errors * errors, axis=1, keepdims=True) + SPARSITY * total[:, COL:COL + 1]
        high = loss.astype(BF16).astype(F32)
        low = loss - high
        lane = lax.broadcasted_iota(jnp.int32, (8, WIDE - COL), 1)
        tail = jnp.where(lane == 0, high, jnp.where(lane == 1, low, 0.0))
        out_ref[:, :, :COL] = jnp.broadcast_to(errors.astype(BF16)[None], (32, 8, COL))
        out_ref[:, :, COL:] = jnp.broadcast_to(tail.astype(BF16)[None], (32, 8, WIDE - COL))

    return pl.pallas_call(
        body,
        out_shape=jax.ShapeDtypeStruct((32, 8, WIDE), BF16),
        compiler_params=params(),
        name="error_rows",
    )(parts, offset)


def decoder_gradient(errors, chunks, order, dec_t, norms):
    def body(order_ref, errors_ref, *refs):
        feats, (dec_ref, norm_ref, out_ref, sum_ref) = refs[:8], refs[8:]
        step = pl.program_id(0)
        for k in range(8):
            @pl.when(step == k)
            def _():
                feat = feats[k][...]
                direct = dot(errors_ref[:, :COL], feat, ((0,), (0,)))
                totals = jnp.sum(feat.astype(F32), axis=0, keepdims=True)
                scale = SPARSITY * totals / norm_ref[...]
                out_ref[...] = (direct + scale * dec_ref[...].astype(F32)).astype(BF16)
                if k == 0:
                    sum_ref[...] = jnp.sum(errors_ref[...].astype(F32), axis=0, keepdims=True)

    block = pl.BlockSpec((COL, CHUNK), lambda i, order: (0, order[i]))
    return pl.pallas_call(
        body,
        grid_spec=pltpu.PrefetchScalarGridSpec(
            num_scalar_prefetch=1,
            grid=(8,),
            in_specs=[whole((TOK, WIDE))] + [whole((TOK, CHUNK))] * 8
            + [block, pl.BlockSpec((1, CHUNK), lambda i, order: (0, order[i]))],
            out_specs=[block, whole((1, WIDE))],
        ),
        out_shape=[jax.ShapeDtypeStruct((COL, LAT), BF16), jax.ShapeDtypeStruct((1, WIDE), F32)],
        compiler_params=params(),
        name="decoder_gradient",
        cost_estimate=pl.CostEstimate(
            flops=2 * TOK * COL * LAT, bytes_accessed=COL * LAT * 4 + TOK * LAT * 2, transcendentals=0
        ),
    )(order, errors, *chunks, dec_t, norms)


def encoder_gradient(act_t, chunks, order):
    def body(order_ref, act_ref, *refs):
        grads, (out_ref, sum_ref) = refs[:8], refs[8:]
        step = pl.program_id(0)
        for k in range(8):
            @pl.when(step == k)
            def _():
                grad = grads[k][...]
                out_ref[...] = dot(act_ref[...], grad, ((1,), (0,))).astype(BF16)
                sum_ref[...] = jnp.sum(grad.astype(F32), axis=0, keepdims=True)

    return pl.pallas_call(
        body,
        grid_spec=pltpu.PrefetchScalarGridSpec(
            num_scalar_prefetch=1,
            grid=(8,),
            in_specs=[whole((COL, TOK))] + [whole((TOK, CHUNK))] * 8,
            out_specs=[
                pl.BlockSpec((COL, CHUNK), lambda i, order: (0, order[i])),
                pl.BlockSpec((1, CHUNK), lambda i, order: (0, order[i])),
            ],
        ),
        out_shape=[jax.ShapeDtypeStruct((COL, LAT), BF16), jax.ShapeDtypeStruct((1, LAT), F32)],
        compiler_params=params(),
        name="encoder_gradient",
        cost_estimate=pl.CostEstimate(
            flops=2 * TOK * COL * LAT, bytes_accessed=COL * LAT * 2 + TOK * LAT * 2, transcendentals=0
        ),
    )(order, act_t, *chunks)


def gather_chunks(own):
    same = [own] + [on_width(own, x_shift(d)) for d in (1, 2, 3)]
    return same + [on_width(chunk, CORE_SWAP) for chunk in same]


def scatter_sums(send, keep, kind):
    pair = [mine + on_width(other, CORE_SWAP).astype(F32) for mine, other in zip(keep, send)]
    total = pair[0]
    for d in (2, 1, 3):
        total = total + on_width(pair[d].astype(kind), x_shift(d)).astype(F32)
    return total


def shards(activations, encoder, latent_bias, decoder, output_bias):
    act_t, dec_t = activations.T, decoder.T
    width_index = lax.axis_index("width")
    latent_index = lax.axis_index("latent")
    x, core = width_index // 2, width_index % 2
    hops = jnp.arange(4, dtype=jnp.int32)
    ahead, behind = (x + hops) % 4 * 2, (x - hops) % 4 * 2
    send_order = (ahead + 1 - core).astype(jnp.int32)
    keep_order = (ahead + core).astype(jnp.int32)
    gathered_order = jnp.concatenate([behind + core, behind + 1 - core]).astype(jnp.int32)
    own = width_index * CHUNK

    send = four_chunks(act_t, encoder, send_order, 0, F32, "preact_send")
    keep = four_chunks(act_t, encoder, keep_order, 0, F32, "preact_keep")
    preact = scatter_sums(send, keep, F32) + lax.dynamic_slice(latent_bias, (own,), (CHUNK,))[None, :]
    features = jnp.maximum(preact, 0.0).astype(BF16)

    squares = jnp.sum(jnp.square(dec_t.astype(F32)), axis=0).reshape(16, 128)
    squares = squares + on_width(squares, CORE_SWAP)
    squares = squares + on_width(squares, X_PAIR_NEAR)
    norms = jnp.sqrt(squares + EPSILON)
    weights = (norms + on_width(norms, X_PAIR_FAR)).reshape(1, LAT)
    own_weights = lax.dynamic_slice(weights, (0, own), (1, CHUNK))

    feature_chunks = gather_chunks(features)
    parts = rebuild(feature_chunks, gathered_order, dec_t, own_weights).reshape(32, 8, WIDE)
    parts = lax.all_to_all(parts, "latent", 0, 0)
    offset = output_bias[None, :] - lax.dynamic_slice(activations, (latent_index * 8, 0), (8, COL)).astype(F32)
    errors = lax.all_to_all(error_rows(parts, offset), "latent", 0, 0).reshape(TOK, WIDE)

    loss = jnp.sum(errors[:, COL:].astype(F32))
    loss = jnp.full((8, 128), loss)
    for pairs in (CORE_SWAP, X_PAIR_NEAR, X_PAIR_FAR):
        loss = loss + on_width(loss, pairs)
    loss_value = loss[0, 0] / (TOK * LAYERS * D)

    send = four_chunks(errors, dec_t, send_order, 1, BF16, "back_send")
    keep = four_chunks(errors, dec_t, keep_order, 1, F32, "back_keep")
    back = scatter_sums(send, keep, BF16)
    grad_pre = jnp.where(features > 0, back + SPARSITY * own_weights, 0.0).astype(BF16)
    decoder_grad, output_grad = decoder_gradient(
        errors, feature_chunks, gathered_order, dec_t, norms.reshape(1, LAT)
    )
    encoder_grad, latent_grad = encoder_gradient(act_t, gather_chunks(grad_pre), gathered_order)
    return (loss_value, encoder_grad, latent_grad[0], decoder_grad.T, output_grad[0, :COL])


def solution(mesh):
    placed = (P(None, "width"), P("width", "latent"), P("latent"), P("latent", "width"), P("width"))
    return jax.shard_map(
        shards,
        mesh=mesh,
        in_specs=placed,
        out_specs=(P(), P("width", "latent"), P("latent"), P("latent", "width"), P("width")),
        check_vma=False,
    )
```

```python
import jax
import jax.numpy as jnp
from jax import lax
from jax.experimental import pallas as pl
from jax.experimental.pallas import tpu as pltpu
from jax.sharding import PartitionSpec as P

D = 2304
LAYERS = 2
SPARSITY = 0.5
EPSILON = 1e-06
F32 = jnp.float32
BF16 = jnp.bfloat16
TOK = 256
COL = 576
CHUNK = 256
WIDE = 640
LAT = 2048
ROWS = TOK + 16
SPAN = 250.0
LOWEST = 125.0
LN2 = 0.6931471805599453
HOPS = (2, 1, 3)
FIRST = 4
VMEM_BYTES = 16 * 1024 * 1024

CORE_SWAP = [(i, i ^ 1) for i in range(8)]


def x_shift(d):
    return [(i, (i + 2 * d) % 8) for i in range(8)]


def on_width(value, pairs):
    return lax.ppermute(value, "width", pairs)


def dot(a, b, dims):
    return lax.dot_general(a, b, (dims, ((), ())), preferred_element_type=F32)


IN_VMEM = pl.BlockSpec(memory_space=pltpu.VMEM)
ANYWHERE = pl.BlockSpec(memory_space=pl.ANY)


def call(body, name, args, in_specs, outs, out_specs=None, scratch=(), flops=0, moved=0):
    return pl.pallas_call(
        body,
        in_specs=in_specs,
        out_specs=out_specs or [IN_VMEM] * len(outs),
        out_shape=[jax.ShapeDtypeStruct(shape, kind) for shape, kind in outs],
        scratch_shapes=list(scratch),
        compiler_params=pltpu.CompilerParams(vmem_limit_bytes=VMEM_BYTES),
        name=name,
        cost_estimate=pl.CostEstimate(flops=flops, bytes_accessed=moved, transcendentals=0),
    )(*args)


def place():
    width_index = lax.axis_index("width")
    return width_index // 2, width_index % 2


def owner(x, core):
    return lax.rem(x + 4, 4) * 2 + core


def gathered_owners():
    x, core = place()
    return [owner(x - d, side) for d in (0, *HOPS) for side in (core, 1 - core)]


def columns(chunk):
    return pl.ds(pl.multiple_of(chunk * CHUNK, CHUNK), CHUNK)


def preact_send(act_t, encoder):
    def body(act_ref, enc_ref, *refs):
        outs, (act_out, act_buf, enc_buf, act_sem, sems) = refs[:4], refs[4:]
        x, core = place()
        act_copy = pltpu.make_async_copy(act_ref, act_buf, act_sem)
        act_copy.start()
        copies = []
        for d in range(4):
            span = columns(owner(x + d, 1 - core))
            copies.append(pltpu.make_async_copy(enc_ref.at[:, span], enc_buf.at[d], sems.at[d]))
            copies[d].start()
        act_copy.wait()
        act = act_buf[...].T
        act_out[...] = act
        for d in range(4):
            copies[d].wait()
            outs[d][...] = dot(act, enc_buf[d], ((1,), (0,)))

    act_t = pltpu.with_memory_space_constraint(act_t, pltpu.HBM)
    encoder = pltpu.with_memory_space_constraint(encoder, pltpu.HBM)
    found = call(
        body, "preact_send", (act_t, encoder), [ANYWHERE] * 2, [((TOK, CHUNK), F32)] * 4 + [((TOK, COL), BF16)],
        scratch=[
            pltpu.VMEM((COL, TOK), BF16), pltpu.VMEM((4, COL, CHUNK), BF16),
            pltpu.SemaphoreType.DMA, pltpu.SemaphoreType.DMA((4,)),
        ],
        flops=8 * TOK * COL * CHUNK, moved=8 * COL * CHUNK + 16 * TOK * CHUNK,
    )
    return found[:4], found[4]


def own_column(left, right, hops, swap, kind, name):
    def body(left_ref, right_ref, *outs):
        x, core = place()
        side = 1 - core if swap else core
        value = left_ref[:, :COL]
        for d, out in zip(hops, outs):
            out[...] = dot(value, right_ref[:, columns(owner(x + d, side))], ((1,), (0,))).astype(kind)

    count = len(hops)
    found = call(
        body, name, (left, right), [IN_VMEM] * 2, [((TOK, CHUNK), kind)] * count,
        flops=2 * count * TOK * COL * CHUNK, moved=2 * count * COL * CHUNK + 2 * count * TOK * CHUNK,
    )
    return dict(zip(hops, found))


def square_sums(dec_t):
    def body(dec_ref, out_ref):
        for chunk in range(8):
            span = slice(chunk * CHUNK, chunk * CHUNK + CHUNK)
            total = jnp.sum(jnp.square(dec_ref[:, span].astype(F32)), axis=0, keepdims=True)
            out_ref[:, span] = jnp.broadcast_to(total, (8, CHUNK))

    return call(body, "square_sums", (dec_t,), [IN_VMEM], [((8, LAT), F32)], flops=2 * COL * LAT, moved=2 * COL * LAT)[0]


def pieces(value, count):
    found = []
    for _ in range(count):
        piece = value.astype(BF16).astype(F32)
        found.append(piece)
        value = value - piece
    return found


def stack_rows(rows):
    index = lax.broadcasted_iota(jnp.int32, (16, rows[0].shape[1]), 0)
    out = jnp.zeros(index.shape, F32)
    for k, row in enumerate(rows):
        out = jnp.where(index == k, row, out)
    return out.astype(BF16)


def encode(mine, other, squares, d):
    def body(mine_ref, other_ref, square_ref, square_other_ref, out_ref):
        x, core = place()
        span = columns(owner(x + d, core))
        value = mine_ref[...] + other_ref[...]
        size = jnp.abs(value)
        largest = jnp.maximum(jnp.max(size, axis=1, keepdims=True), 1e-30) * (1.0 + 2.0 ** -7)
        largest = largest.astype(BF16).astype(F32)
        power = jnp.exp2(size * (SPAN / largest) - LOWEST)
        out_ref[:TOK] = jnp.where(value < 0, -power, power).astype(BF16)
        scale = jnp.broadcast_to(largest, (TOK, 128)).T[:1]
        out_ref[TOK:] = stack_rows([scale] + pieces(square_ref[:1, span] + square_other_ref[:1, span], 3))

    return call(
        body, "encode_sums", (mine, other, *squares), [IN_VMEM] * 4, [((ROWS, CHUNK), BF16)], moved=6 * TOK * CHUNK
    )[0]


def decode(ref):
    scale = jnp.broadcast_to(ref[TOK:TOK + 1].astype(F32), (128, TOK)).T[:, :1]
    power = ref[:TOK].astype(F32)
    size = (jnp.log(jnp.abs(power)) * (1.0 / LN2) + LOWEST) * (scale * (1.0 / SPAN))
    rows = ref[TOK:].astype(F32)
    return jnp.where(power < 0, -size, size), rows[1:2] + rows[2:3] + rows[3:4]


def own_features(mine, other, parts, squares, latent_bias):
    def body(mine_ref, other_ref, *refs):
        part_refs, (square_ref, square_other_ref, bias_ref, out_ref, weight_ref) = refs[:3], refs[3:]
        x, core = place()
        span = columns(owner(x, core))
        preact = mine_ref[...] + other_ref[...] + bias_ref[:, span]
        sources = [square_ref[:1, span] + square_other_ref[:1, span]]
        for ref in part_refs:
            value, square = decode(ref)
            preact += value
            sources.append(square)
        sums = [jnp.zeros((1, CHUNK), F32) for _ in range(LAYERS)]
        for d, square in zip((0, *HOPS), sources):
            layer = lax.rem(x - d + 4, 4) // 2
            sums = [have + jnp.where(layer == k, square, 0.0) for k, have in enumerate(sums)]
        norms = [jnp.sqrt(have + EPSILON) for have in sums]
        weight_ref[...] = jnp.broadcast_to(norms[0] + norms[1], (8, CHUNK))
        out_ref[:TOK] = jnp.maximum(preact, 0.0).astype(BF16)
        out_ref[TOK:] = stack_rows(pieces(norms[0], 3) + pieces(norms[1], 3))

    return call(
        body, "own_features", (mine, other, *parts, *squares, latent_bias), [IN_VMEM] * 8,
        [((ROWS, CHUNK), BF16), ((8, CHUNK), F32)], moved=16 * TOK * CHUNK,
    )


def rebuild_first(chunks, dec_t, own_weights):
    def body(*refs):
        feats, (dec_ref, weight_ref, out_ref) = refs[:FIRST], refs[FIRST:]
        acc = jnp.zeros((TOK, COL), F32)
        for feat, chunk in zip(feats, gathered_owners()):
            acc += dot(feat[:TOK], dec_ref[:, columns(chunk)], ((1,), (1,)))
        penalty = jnp.sum(feats[0][:TOK].astype(F32) * weight_ref[:1], axis=1, keepdims=True)
        out_ref[:, :COL] = acc
        out_ref[:, COL:] = jnp.broadcast_to(penalty, (TOK, WIDE - COL))

    return call(
        body, "rebuild_first", (*chunks, dec_t, own_weights), [IN_VMEM] * (FIRST + 2), [((TOK, WIDE), F32)],
        flops=2 * TOK * COL * CHUNK * FIRST, moved=2 * COL * LAT + 2 * TOK * LAT,
    )[0]


def rebuild_last(chunks, dec_t, partial):
    def body(*refs):
        feats, (dec_ref, partial_ref, out_ref) = refs[:8 - FIRST], refs[8 - FIRST:]
        acc = partial_ref[:, :COL]
        for feat, chunk in zip(feats, gathered_owners()[FIRST:]):
            acc += dot(feat[:TOK], dec_ref[:, columns(chunk)], ((1,), (1,)))
        out_ref[:, :COL] = acc.astype(BF16)
        out_ref[:, COL:] = partial_ref[:, COL:].astype(BF16)

    return call(
        body, "rebuild_last", (*chunks, dec_t, partial), [IN_VMEM] * (10 - FIRST), [((TOK, WIDE), BF16)],
        flops=2 * TOK * COL * CHUNK * (8 - FIRST), moved=2 * COL * LAT + 2 * TOK * LAT,
    )[0]


def error_rows(parts, act_t, output_bias):
    def body(parts_ref, act_ref, bias_ref, out_ref):
        first = lax.axis_index("latent") * 8
        token = lax.broadcasted_iota(jnp.int32, (8, TOK), 1)
        wanted = lax.broadcasted_iota(jnp.int32, (8, TOK), 0) + first
        pick = jnp.where(token == wanted, 1.0, 0.0).astype(BF16)
        act = dot(pick, act_ref[...], ((1,), (1,)))
        total = jnp.sum(parts_ref[...].astype(F32), axis=0)
        errors = total[:, :COL] + bias_ref[...] - act
        loss = 0.5 * jnp.sum(errors * errors, axis=1, keepdims=True) + SPARSITY * total[:, COL:COL + 1]
        lane = lax.broadcasted_iota(jnp.int32, (8, WIDE - COL), 1)
        tail = jnp.zeros((8, WIDE - COL), F32)
        for k, piece in enumerate(pieces(loss, 3)):
            tail = jnp.where(lane == k, piece, tail)
        out_ref[:, :, :COL] = jnp.broadcast_to(errors.astype(BF16)[None], (32, 8, COL))
        out_ref[:, :, COL:] = jnp.broadcast_to(tail.astype(BF16)[None], (32, 8, WIDE - COL))

    return call(
        body, "error_rows", (parts, act_t, output_bias), [IN_VMEM] * 3, [((32, 8, WIDE), BF16)], moved=4 * TOK * WIDE
    )[0]


def own_gradient(mine, other, parts, features, weights, errors):
    def body(mine_ref, other_ref, one_ref, two_ref, three_ref, feat_ref, weight_ref, tail_ref, out_ref):
        total = mine_ref[...] + other_ref[...].astype(F32)
        for ref in (one_ref, two_ref, three_ref):
            total += ref[...].astype(F32)
        total += SPARSITY * weight_ref[:1]
        out_ref[:TOK] = jnp.where(feat_ref[:TOK].astype(F32) > 0, total, 0.0).astype(BF16)
        loss = jnp.sum(jnp.sum(tail_ref[:, COL:].astype(F32), axis=0, keepdims=True), axis=1, keepdims=True)
        out_ref[TOK:] = stack_rows([jnp.broadcast_to(piece, (1, CHUNK)) for piece in pieces(loss, 3)])

    return call(
        body, "own_gradient", (mine, other, *parts, features, weights, errors), [IN_VMEM] * 8,
        [((ROWS, CHUNK), BF16)], moved=16 * TOK * CHUNK,
    )[0]


def store_chunks(values, owners, out_ref, buffer, sems):
    copies = []
    for k, chunk in enumerate(owners):
        buffer[k] = values(k, chunk)
        copies.append(pltpu.make_async_copy(buffer.at[k], out_ref.at[:, columns(chunk)], sems.at[k]))
        copies[-1].start()
    for copy in copies:
        copy.wait()


def decoder_gradient(errors, chunks, dec_t):
    def body(errors_ref, *refs):
        feats, (dec_ref, out_ref, sum_ref, buffer, sems) = refs[:8], refs[8:]
        x, _ = place()
        layer = x // 2
        error = errors_ref[:, :COL].T

        def values(k, chunk):
            feat = feats[k][:TOK]
            rows = feats[k][TOK:].astype(F32)
            norm = jnp.where(layer == 0, rows[0:1] + rows[1:2] + rows[2:3], rows[3:4] + rows[4:5] + rows[5:6])
            totals = jnp.sum(feat.astype(F32), axis=0, keepdims=True)
            scale = SPARSITY * totals / norm
            return (dot(error, feat, ((1,), (0,))) + scale * dec_ref[:, columns(chunk)].astype(F32)).astype(BF16)

        store_chunks(values, gathered_owners(), out_ref, buffer, sems)
        sum_ref[...] = jnp.sum(errors_ref[:, :COL].astype(F32), axis=0, keepdims=True)

    return call(
        body, "decoder_gradient", (errors, *chunks, dec_t), [IN_VMEM] * 10,
        [((COL, LAT), BF16), ((1, COL), F32)], out_specs=[ANYWHERE, IN_VMEM],
        scratch=[pltpu.VMEM((8, COL, CHUNK), BF16), pltpu.SemaphoreType.DMA((8,))],
        flops=2 * TOK * COL * LAT, moved=4 * COL * LAT + 2 * TOK * LAT,
    )


def loss_rows(grads):
    loss = jnp.zeros((1, 128), F32)
    for grad in grads:
        rows = grad[TOK:, :128].astype(F32)
        loss += rows[0:1] + rows[1:2] + rows[2:3]
    return loss * (1.0 / (TOK * LAYERS * D))


def encoder_gradient(act_t, chunks, start, before=None):
    count = len(chunks)

    def body(act_ref, *refs):
        grads, (out_ref, sum_ref, loss_ref, buffer, sems) = refs[:count], refs[-5:]
        owners = gathered_owners()[start:start + count]
        if before is None:
            sum_ref[...] = jnp.zeros((1, LAT), F32)
            loss_ref[...] = loss_rows(grads)
        else:
            sum_ref[...] = refs[count + 1][...]
            loss_ref[...] = refs[count + 2][...] + loss_rows(grads)

        def values(k, chunk):
            grad = grads[k][:TOK]
            sum_ref[:, columns(chunk)] = jnp.sum(grad.astype(F32), axis=0, keepdims=True)
            return dot(act_ref[...], grad, ((1,), (0,))).astype(BF16)

        store_chunks(values, owners, out_ref, buffer, sems)

    extra = () if before is None else tuple(before)
    return pl.pallas_call(
        body,
        in_specs=[IN_VMEM] * (1 + count) + [ANYWHERE, IN_VMEM, IN_VMEM][:len(extra)],
        out_specs=[ANYWHERE, IN_VMEM, IN_VMEM],
        out_shape=[
            jax.ShapeDtypeStruct((COL, LAT), BF16), jax.ShapeDtypeStruct((1, LAT), F32),
            jax.ShapeDtypeStruct((1, 128), F32),
        ],
        scratch_shapes=[pltpu.VMEM((count, COL, CHUNK), BF16), pltpu.SemaphoreType.DMA((count,))],
        input_output_aliases={1 + count: 0} if extra else {},
        compiler_params=pltpu.CompilerParams(vmem_limit_bytes=VMEM_BYTES),
        name="encoder_gradient_last" if extra else "encoder_gradient_first",
        cost_estimate=pl.CostEstimate(
            flops=2 * TOK * COL * CHUNK * count, bytes_accessed=2 * COL * CHUNK * count, transcendentals=0
        ),
    )(act_t, *chunks, *extra)


def gather_chunks(own, work):
    moved = [on_width(own, x_shift(d)) for d in HOPS]
    first = [chunk for part in (own, moved[0]) for chunk in (part, on_width(part, CORE_SWAP))]
    done = work(first)
    return first + [chunk for part in moved[1:] for chunk in (part, on_width(part, CORE_SWAP))], done


def shards(activations, encoder, latent_bias, decoder, output_bias):
    act_t, dec_t = activations.T, decoder.T

    send, act = preact_send(act_t, encoder)
    swapped = {d: on_width(send[d], CORE_SWAP) for d in (*HOPS, 0)}
    keep = own_column(act, encoder, (*HOPS, 0), False, F32, "preact_keep")
    squares = square_sums(dec_t)
    squares = (squares, on_width(squares, CORE_SWAP))
    coded = [on_width(encode(keep[d], swapped[d], squares, d), x_shift(d)) for d in HOPS]
    features, own_weights = own_features(keep[0], swapped[0], coded, squares, latent_bias[None, :])

    feature_chunks, partial = gather_chunks(features, lambda chunks: rebuild_first(chunks, dec_t, own_weights))
    parts = rebuild_last(feature_chunks[FIRST:], dec_t, partial).reshape(32, 8, WIDE)
    parts, bias_row = lax.optimization_barrier((parts, output_bias[None, :]))
    parts = lax.all_to_all(parts, "latent", 0, 0)
    errors = error_rows(parts, act_t, bias_row)
    errors = lax.all_to_all(errors, "latent", 0, 0).reshape(TOK, WIDE)

    far, rest = HOPS[:1], (*HOPS[1:], 0)
    send = own_column(errors, dec_t, far, True, BF16, "back_send_far")
    swapped = {d: on_width(send[d], CORE_SWAP) for d in far}
    keep = own_column(errors, dec_t, far, False, F32, "back_keep_far")
    send = own_column(errors, dec_t, rest, True, BF16, "back_send")
    swapped |= {d: on_width(send[d], CORE_SWAP) for d in rest}
    keep |= own_column(errors, dec_t, rest, False, F32, "back_keep")
    summed = [on_width((keep[d] + swapped[d].astype(F32)).astype(BF16), x_shift(d)) for d in HOPS]
    decoder_grad, output_grad = decoder_gradient(errors, feature_chunks, dec_t)
    decoder_grad, output_grad, features = lax.optimization_barrier((decoder_grad, output_grad[0], features))
    grad_pre = own_gradient(keep[0], swapped[0], summed, features, own_weights, errors)
    grad_chunks, first = gather_chunks(grad_pre, lambda chunks: encoder_gradient(act_t, chunks, 0))
    encoder_grad, latent_grad, loss_value = encoder_gradient(act_t, grad_chunks[FIRST:], FIRST, first)
    return (loss_value[0, 0], encoder_grad, latent_grad[0], decoder_grad.T, output_grad)


def solution(mesh):
    placed = (P(None, "width"), P("width", "latent"), P("latent"), P("latent", "width"), P("width"))
    return jax.shard_map(
        shards,
        mesh=mesh,
        in_specs=placed,
        out_specs=(P(), P("width", "latent"), P("latent"), P("latent", "width"), P("width")),
        check_vma=False,
    )
```

```python
import jax
import jax.numpy as jnp
from jax import lax
from jax.experimental import pallas as pl
from jax.experimental.pallas import tpu as pltpu
from jax.sharding import PartitionSpec as P

D = 2304
LAYERS = 2
SPARSITY = 0.5
EPSILON = 1e-06
F32 = jnp.float32
BF16 = jnp.bfloat16
TOK = 256
COL = 576
CHUNK = 256
WIDE = 640
LAT = 2048
ROWS = TOK + 16
SPAN = 250.0
LOWEST = 125.0
LN2 = 0.6931471805599453
FAR = 2
HOPS = (FAR, 1, 3)
BACKWARD = HOPS[::-1]
REST = (1, 3, 0)
FIRST_REBUILD = 4
VMEM_BYTES = 16 * 1024 * 1024

CORE_SWAP = [(i, i ^ 1) for i in range(8)]


def x_shift(d):
    return [(i, (i + 2 * d) % 8) for i in range(8)]


def on_width(value, pairs):
    return lax.ppermute(value, "width", pairs)


def dot(a, b, dims):
    return lax.dot_general(a, b, (dims, ((), ())), preferred_element_type=F32)


IN_VMEM = pl.BlockSpec(memory_space=pltpu.VMEM)
ANYWHERE = pl.BlockSpec(memory_space=pl.ANY)


def call(body, name, args, in_specs, outs, out_specs=None, scratch=(), flops=0, moved=0):
    return pl.pallas_call(
        body,
        in_specs=in_specs,
        out_specs=out_specs or [IN_VMEM] * len(outs),
        out_shape=[jax.ShapeDtypeStruct(shape, kind) for shape, kind in outs],
        scratch_shapes=list(scratch),
        compiler_params=pltpu.CompilerParams(vmem_limit_bytes=VMEM_BYTES),
        name=name,
        cost_estimate=pl.CostEstimate(flops=flops, bytes_accessed=moved, transcendentals=0),
    )(*args)


def place():
    width_index = lax.axis_index("width")
    return width_index // 2, width_index % 2


def owner(x, core):
    return lax.rem(x + 4, 4) * 2 + core


def gathered_owners(hops=HOPS):
    x, core = place()
    return [owner(x - d, side) for d in (0, *hops) for side in (core, 1 - core)]


def columns(chunk):
    return pl.ds(pl.multiple_of(chunk * CHUNK, CHUNK), CHUNK)


def preact_far(act_t, encoder):
    def body(act_ref, enc_ref, send_ref, keep_ref, act_out, enc_out, act_buf, act_sem, sems):
        x, core = place()
        act_copy = pltpu.make_async_copy(act_ref, act_buf, act_sem)
        act_copy.start()
        spans = [columns(owner(x + d, side)) for d in (FAR, *REST) for side in (1 - core, core)]
        copies = []
        for k, span in enumerate(spans):
            copies.append(pltpu.make_async_copy(enc_ref.at[:, span], enc_out.at[:, span], sems.at[k]))
            copies[k].start()
        act_copy.wait()
        act = act_buf[...].T
        act_out[...] = act
        for copy, span, out in zip(copies, spans, (send_ref, keep_ref)):
            copy.wait()
            out[...] = dot(act, enc_out[:, span], ((1,), (0,)))
        for copy in copies[2:]:
            copy.wait()

    act_t = pltpu.with_memory_space_constraint(act_t, pltpu.HBM)
    encoder = pltpu.with_memory_space_constraint(encoder, pltpu.HBM)
    return call(
        body, "preact_far", (act_t, encoder), [ANYWHERE] * 2,
        [((TOK, CHUNK), F32)] * 2 + [((TOK, COL), BF16), ((COL, LAT), BF16)],
        scratch=[pltpu.VMEM((COL, TOK), BF16), pltpu.SemaphoreType.DMA, pltpu.SemaphoreType.DMA((8,))],
        flops=2_400_000_000, moved=4 * COL * CHUNK + 8 * TOK * CHUNK,
    )


def back_far(errors, dec_t):
    def body(errors_ref, dec_ref, send_ref, keep_ref):
        x, core = place()
        value = errors_ref[:, :COL]
        send_ref[...] = dot(value, dec_ref[:, columns(owner(x + FAR, 1 - core))], ((1,), (0,))).astype(BF16)
        keep_ref[...] = dot(value, dec_ref[:, columns(owner(x + FAR, core))], ((1,), (0,)))

    return call(
        body, "back_far", (errors, dec_t), [IN_VMEM] * 2, [((TOK, CHUNK), BF16), ((TOK, CHUNK), F32)],
        flops=4 * TOK * COL * CHUNK, moved=4 * COL * CHUNK + 6 * TOK * CHUNK,
    )


def rest_parts(left, right, swap, kind, name):
    def body(left_ref, right_ref, out):
        x, core = place()
        side = 1 - core if swap else core
        value = left_ref[:, :COL]
        for k, d in enumerate(REST):
            part = dot(value, right_ref[:, columns(owner(x + d, side))], ((1,), (0,)))
            out[k * TOK:(k + 1) * TOK] = part.astype(kind)

    return call(
        body, name, (left, right), [IN_VMEM] * 2, [((3 * TOK, CHUNK), kind)],
        flops=6 * TOK * COL * CHUNK, moved=6 * COL * CHUNK + 6 * TOK * CHUNK,
    )[0]


def rows_of(d):
    first = 0 if d == FAR else REST.index(d) * TOK
    return slice(first, first + TOK)


def square_sums(dec_t):
    def body(dec_ref, out_ref):
        for chunk in range(8):
            span = slice(chunk * CHUNK, chunk * CHUNK + CHUNK)
            total = jnp.sum(jnp.square(dec_ref[:, span].astype(F32)), axis=0, keepdims=True)
            out_ref[:, span] = jnp.broadcast_to(total, (8, CHUNK))

    return call(body, "square_sums", (dec_t,), [IN_VMEM], [((8, LAT), F32)], flops=2 * COL * LAT, moved=2 * COL * LAT)[0]


def pieces(value, count):
    found = []
    for _ in range(count):
        piece = value.astype(BF16).astype(F32)
        found.append(piece)
        value = value - piece
    return found


def stack_rows(rows):
    index = lax.broadcasted_iota(jnp.int32, (16, rows[0].shape[1]), 0)
    out = jnp.zeros(index.shape, F32)
    for k, row in enumerate(rows):
        out = jnp.where(index == k, row, out)
    return out.astype(BF16)


def encode(mine, other, squares, d):
    def body(mine_ref, other_ref, square_ref, square_other_ref, out_ref):
        x, core = place()
        span = columns(owner(x + d, core))
        value = mine_ref[rows_of(d)] + other_ref[rows_of(d)]
        size = jnp.abs(value)
        largest = jnp.maximum(jnp.max(size, axis=1, keepdims=True), 1e-30) * (1.0 + 2.0 ** -7)
        largest = largest.astype(BF16).astype(F32)
        power = jnp.exp2(size * (SPAN / largest) - LOWEST)
        out_ref[:TOK] = jnp.where(value < 0, -power, power).astype(BF16)
        scale = jnp.broadcast_to(largest, (TOK, 128)).T[:1]
        out_ref[TOK:] = stack_rows([scale] + pieces(square_ref[:1, span] + square_other_ref[:1, span], 3))

    return call(
        body, "encode_sums", (mine, other, *squares), [IN_VMEM] * 4, [((ROWS, CHUNK), BF16)], moved=6 * TOK * CHUNK
    )[0]


def decode(ref):
    scale = jnp.broadcast_to(ref[TOK:TOK + 1].astype(F32), (128, TOK)).T[:, :1]
    power = ref[:TOK].astype(F32)
    size = (jnp.log(jnp.abs(power)) * (1.0 / LN2) + LOWEST) * (scale * (1.0 / SPAN))
    rows = ref[TOK:].astype(F32)
    return jnp.where(power < 0, -size, size), rows[1:2] + rows[2:3] + rows[3:4]


def own_features(mine, other, parts, squares, latent_bias):
    def body(mine_ref, other_ref, *refs):
        part_refs, (square_ref, square_other_ref, bias_ref, out_ref, weight_ref) = refs[:3], refs[3:]
        x, core = place()
        span = columns(owner(x, core))
        preact = mine_ref[rows_of(0)] + other_ref[rows_of(0)] + bias_ref[:, span]
        sources = [square_ref[:1, span] + square_other_ref[:1, span]]
        for ref in part_refs:
            value, square = decode(ref)
            preact += value
            sources.append(square)
        sums = [jnp.zeros((1, CHUNK), F32) for _ in range(LAYERS)]
        for d, square in zip((0, *HOPS), sources):
            layer = lax.rem(x - d + 4, 4) // 2
            sums = [have + jnp.where(layer == k, square, 0.0) for k, have in enumerate(sums)]
        norms = [jnp.sqrt(have + EPSILON) for have in sums]
        weight_ref[...] = jnp.broadcast_to(norms[0] + norms[1], (8, CHUNK))
        out_ref[:TOK] = jnp.maximum(preact, 0.0).astype(BF16)
        out_ref[TOK:] = stack_rows(pieces(norms[0], 3) + pieces(norms[1], 3))

    return call(
        body, "own_features", (mine, other, *parts, *squares, latent_bias), [IN_VMEM] * 8,
        [((ROWS, CHUNK), BF16), ((8, CHUNK), F32)], moved=16 * TOK * CHUNK,
    )


def rebuild_first(chunks, dec_t, own_weights):
    def body(*refs):
        feats, (dec_ref, weight_ref, out_ref) = refs[:FIRST_REBUILD], refs[FIRST_REBUILD:]
        acc = jnp.zeros((TOK, COL), F32)
        for feat, chunk in zip(feats, gathered_owners()):
            acc += dot(feat[:TOK], dec_ref[:, columns(chunk)], ((1,), (1,)))
        penalty = jnp.sum(feats[0][:TOK].astype(F32) * weight_ref[:1], axis=1, keepdims=True)
        out_ref[:, :COL] = acc
        out_ref[:, COL:] = jnp.broadcast_to(penalty, (TOK, WIDE - COL))

    return call(
        body, "rebuild_first", (*chunks, dec_t, own_weights), [IN_VMEM] * (FIRST_REBUILD + 2), [((TOK, WIDE), F32)],
        flops=2 * TOK * COL * CHUNK * FIRST_REBUILD, moved=2 * COL * LAT + 2 * TOK * LAT,
    )[0]


def rebuild_last(chunks, dec_t, partial):
    def body(*refs):
        feats, (dec_ref, partial_ref, out_ref) = refs[:8 - FIRST_REBUILD], refs[8 - FIRST_REBUILD:]
        acc = partial_ref[:, :COL]
        for feat, chunk in zip(feats, gathered_owners()[FIRST_REBUILD:]):
            acc += dot(feat[:TOK], dec_ref[:, columns(chunk)], ((1,), (1,)))
        out_ref[:, :COL] = acc.astype(BF16)
        out_ref[:, COL:] = partial_ref[:, COL:].astype(BF16)

    return call(
        body, "rebuild_last", (*chunks, dec_t, partial), [IN_VMEM] * (10 - FIRST_REBUILD), [((TOK, WIDE), BF16)],
        flops=2 * TOK * COL * CHUNK * (8 - FIRST_REBUILD), moved=2 * COL * LAT + 2 * TOK * LAT,
    )[0]


def error_rows(parts, act_t, output_bias):
    def body(parts_ref, act_ref, bias_ref, out_ref):
        first = lax.axis_index("latent") * 8
        token = lax.broadcasted_iota(jnp.int32, (8, TOK), 1)
        wanted = lax.broadcasted_iota(jnp.int32, (8, TOK), 0) + first
        pick = jnp.where(token == wanted, 1.0, 0.0).astype(BF16)
        act = dot(pick, act_ref[...], ((1,), (1,)))
        total = jnp.sum(parts_ref[...].astype(F32), axis=0)
        errors = total[:, :COL] + bias_ref[...] - act
        loss = 0.5 * jnp.sum(errors * errors, axis=1, keepdims=True) + SPARSITY * total[:, COL:COL + 1]
        lane = lax.broadcasted_iota(jnp.int32, (8, WIDE - COL), 1)
        tail = jnp.zeros((8, WIDE - COL), F32)
        for k, piece in enumerate(pieces(loss, 3)):
            tail = jnp.where(lane == k, piece, tail)
        out_ref[:, :, :COL] = jnp.broadcast_to(errors.astype(BF16)[None], (32, 8, COL))
        out_ref[:, :, COL:] = jnp.broadcast_to(tail.astype(BF16)[None], (32, 8, WIDE - COL))

    return call(
        body, "error_rows", (parts, act_t, output_bias), [IN_VMEM] * 3, [((32, 8, WIDE), BF16)], moved=4 * TOK * WIDE
    )[0]


def own_gradient(mine, other, parts, features, weights, errors):
    def body(mine_ref, other_ref, one_ref, two_ref, three_ref, feat_ref, weight_ref, tail_ref, out_ref):
        total = mine_ref[rows_of(0)] + other_ref[rows_of(0)].astype(F32)
        for ref in (one_ref, two_ref, three_ref):
            total += ref[...].astype(F32)
        total += SPARSITY * weight_ref[:1]
        out_ref[:TOK] = jnp.where(feat_ref[:TOK].astype(F32) > 0, total, 0.0).astype(BF16)
        loss = jnp.sum(jnp.sum(tail_ref[:, COL:].astype(F32), axis=0, keepdims=True), axis=1, keepdims=True)
        out_ref[TOK:] = stack_rows([jnp.broadcast_to(piece, (1, CHUNK)) for piece in pieces(loss, 3)])

    return call(
        body, "own_gradient", (mine, other, *parts, features, weights, errors), [IN_VMEM] * 8,
        [((ROWS, CHUNK), BF16)], moved=16 * TOK * CHUNK,
    )[0]


def store_chunks(values, owners, out_ref, buffer, sems):
    copies = []
    for k, chunk in enumerate(owners):
        buffer[k] = values(k, chunk)
        copies.append(pltpu.make_async_copy(buffer.at[k], out_ref.at[:, columns(chunk)], sems.at[k]))
        copies[-1].start()
    for copy in copies:
        copy.wait()


def decoder_gradient(errors, chunks, dec_t):
    def body(errors_ref, *refs):
        feats, (dec_ref, out_ref, sum_ref, buffer, sems) = refs[:8], refs[8:]
        x, _ = place()
        layer = x // 2
        error = errors_ref[:, :COL].T

        def values(k, chunk):
            feat = feats[k][:TOK]
            rows = feats[k][TOK:].astype(F32)
            norm = jnp.where(layer == 0, rows[0:1] + rows[1:2] + rows[2:3], rows[3:4] + rows[4:5] + rows[5:6])
            totals = jnp.sum(feat.astype(F32), axis=0, keepdims=True)
            scale = SPARSITY * totals / norm
            return (dot(error, feat, ((1,), (0,))) + scale * dec_ref[:, columns(chunk)].astype(F32)).astype(BF16)

        store_chunks(values, gathered_owners(), out_ref, buffer, sems)
        sum_ref[...] = jnp.sum(errors_ref[:, :COL].astype(F32), axis=0, keepdims=True)

    return call(
        body, "decoder_gradient", (errors, *chunks, dec_t), [IN_VMEM] * 10,
        [((COL, LAT), BF16), ((1, COL), F32)], out_specs=[ANYWHERE, IN_VMEM],
        scratch=[pltpu.VMEM((8, COL, CHUNK), BF16), pltpu.SemaphoreType.DMA((8,))],
        flops=2 * TOK * COL * LAT, moved=4 * COL * LAT + 2 * TOK * LAT,
    )


def loss_rows(grads):
    loss = jnp.zeros((1, 128), F32)
    for grad in grads:
        rows = grad[TOK:, :128].astype(F32)
        loss += rows[0:1] + rows[1:2] + rows[2:3]
    return loss * (1.0 / (TOK * LAYERS * D))


def encoder_gradient(act_t, chunks):
    def body(act_ref, *refs):
        grads, (out_ref, sum_ref, loss_ref, buffer, sum_buf, loss_buf, sems, small_sems) = refs[:8], refs[8:]
        loss_buf[...] = loss_rows(grads)
        for grad, chunk in zip(grads, gathered_owners(BACKWARD)):
            sum_buf[:, columns(chunk)] = jnp.sum(grad[:TOK].astype(F32), axis=0, keepdims=True)
        small = [
            pltpu.make_async_copy(sum_buf, sum_ref, small_sems.at[0]),
            pltpu.make_async_copy(loss_buf, loss_ref, small_sems.at[1]),
        ]
        for copy in small:
            copy.start()
        store_chunks(
            lambda k, chunk: dot(act_ref[...], grads[k][:TOK], ((1,), (0,))).astype(BF16),
            gathered_owners(BACKWARD), out_ref, buffer, sems,
        )
        for copy in small:
            copy.wait()

    return call(
        body, "encoder_gradient", (act_t, *chunks), [IN_VMEM] * 9,
        [((COL, LAT), BF16), ((1, LAT), F32), ((1, 128), F32)], out_specs=[ANYWHERE] * 3,
        scratch=[
            pltpu.VMEM((8, COL, CHUNK), BF16), pltpu.VMEM((1, LAT), F32), pltpu.VMEM((1, 128), F32),
            pltpu.SemaphoreType.DMA((8,)), pltpu.SemaphoreType.DMA((2,)),
        ],
        flops=2 * TOK * COL * LAT, moved=2 * COL * LAT + 2 * TOK * LAT,
    )


def gather_chunks(own, hops):
    moved = [own] + [on_width(own, x_shift(d)) for d in hops]
    return [chunk for part in moved for chunk in (part, on_width(part, CORE_SWAP))]


def shards(activations, encoder, latent_bias, decoder, output_bias):
    act_t, dec_t = activations.T, decoder.T

    send, keep_far, act, enc = preact_far(act_t, encoder)
    send, early_dec = lax.optimization_barrier((send, dec_t))
    squares = square_sums(early_dec)
    squares = (squares, on_width(squares, CORE_SWAP))
    far = (keep_far, on_width(send, CORE_SWAP))
    send = rest_parts(act, enc, True, F32, "preact_send")
    keep = rest_parts(act, enc, False, F32, "preact_keep")
    coded, send, keep = lax.optimization_barrier((encode(*far, squares, FAR), send, keep))
    rest = (keep, on_width(send, CORE_SWAP))
    coded = [on_width(coded, x_shift(FAR))] + [on_width(encode(*rest, squares, d), x_shift(d)) for d in HOPS[1:]]
    features, own_weights = own_features(*rest, coded, squares, latent_bias[None, :])

    feature_chunks = gather_chunks(features, HOPS)
    partial = rebuild_first(feature_chunks[:FIRST_REBUILD], dec_t, own_weights)
    parts = rebuild_last(feature_chunks[FIRST_REBUILD:], dec_t, partial).reshape(32, 8, WIDE)
    parts, bias_row = lax.optimization_barrier((parts, output_bias[None, :]))
    parts = lax.all_to_all(parts, "latent", 0, 0)
    errors = error_rows(parts, act_t, bias_row)
    errors = lax.all_to_all(errors, "latent", 0, 0).reshape(TOK, WIDE)

    send, keep_far = back_far(errors, dec_t)
    send, keep_far, errors = lax.optimization_barrier((send, keep_far, errors))
    summed = keep_far + on_width(send, CORE_SWAP).astype(F32)
    send = rest_parts(errors, dec_t, True, BF16, "back_send")
    keep = rest_parts(errors, dec_t, False, F32, "back_keep")
    summed, send, keep = lax.optimization_barrier((summed.astype(BF16), send, keep))
    summed = [on_width(summed, x_shift(FAR))]
    rest = (keep, on_width(send, CORE_SWAP))
    for d in HOPS[1:]:
        total = rest[0][rows_of(d)] + rest[1][rows_of(d)].astype(F32)
        summed.append(on_width(total.astype(BF16), x_shift(d)))
    decoder_grad, output_grad = decoder_gradient(errors, feature_chunks, dec_t)
    decoder_grad, output_grad, features = lax.optimization_barrier((decoder_grad, output_grad[0], features))
    grad_pre = own_gradient(*rest, summed, features, own_weights, errors)
    encoder_grad, latent_grad, loss_value = encoder_gradient(act_t, gather_chunks(grad_pre, BACKWARD))
    return (loss_value[0, 0], encoder_grad, latent_grad[0], decoder_grad.T, output_grad)


def solution(mesh):
    placed = (P(None, "width"), P("width", "latent"), P("latent"), P("latent", "width"), P("width"))
    return jax.shard_map(
        shards,
        mesh=mesh,
        in_specs=placed,
        out_specs=(P(), P("width", "latent"), P("latent"), P("latent", "width"), P("width")),
        check_vma=False,
    )
```

```python
import jax
import jax.numpy as jnp
from jax import lax
from jax.experimental import pallas as pl
from jax.experimental.pallas import tpu as pltpu
from jax.sharding import PartitionSpec as P

D = 2304
LAYERS = 2
SPARSITY = 0.5
EPSILON = 1e-06
F32 = jnp.float32
BF16 = jnp.bfloat16
TOK = 256
COL = 576
CHUNK = 256
WIDE = 640
LAT = 2048
ROWS = TOK + 16
SPAN = 250.0
LOWEST = 125.0
LN2 = 0.6931471805599453
FAR = 2
HOPS = (FAR, 1, 3)
BACKWARD = HOPS[::-1]
REST = (1, 3, 0)
FIRST_REBUILD = 4
VMEM_BYTES = 16 * 1024 * 1024

CORE_SWAP = [(i, i ^ 1) for i in range(8)]


def x_shift(d):
    return [(i, (i + 2 * d) % 8) for i in range(8)]


def on_width(value, pairs):
    return lax.ppermute(value, "width", pairs)


def dot(a, b, dims):
    return lax.dot_general(a, b, (dims, ((), ())), preferred_element_type=F32)


IN_VMEM = pl.BlockSpec(memory_space=pltpu.VMEM)
ANYWHERE = pl.BlockSpec(memory_space=pl.ANY)


def call(body, name, args, in_specs, outs, out_specs=None, scratch=(), flops=0, moved=0):
    return pl.pallas_call(
        body,
        in_specs=in_specs,
        out_specs=out_specs or [IN_VMEM] * len(outs),
        out_shape=[jax.ShapeDtypeStruct(shape, kind) for shape, kind in outs],
        scratch_shapes=list(scratch),
        compiler_params=pltpu.CompilerParams(vmem_limit_bytes=VMEM_BYTES),
        name=name,
        cost_estimate=pl.CostEstimate(flops=flops, bytes_accessed=moved, transcendentals=0),
    )(*args)


def place():
    width_index = lax.axis_index("width")
    return width_index // 2, width_index % 2


def owner(x, core):
    return lax.rem(x + 4, 4) * 2 + core


def gathered_owners(hops=HOPS):
    x, core = place()
    return [owner(x - d, side) for d in (0, *hops) for side in (core, 1 - core)]


def columns(chunk):
    return pl.ds(pl.multiple_of(chunk * CHUNK, CHUNK), CHUNK)


def preact_far(act_t, encoder):
    def body(act_ref, enc_ref, send_ref, keep_ref, act_out, enc_out, act_buf, act_sem, sems):
        x, core = place()
        act_copy = pltpu.make_async_copy(act_ref, act_buf, act_sem)
        act_copy.start()
        spans = [columns(owner(x + d, side)) for d in (FAR, *REST) for side in (1 - core, core)]
        copies = []
        for k, span in enumerate(spans):
            copies.append(pltpu.make_async_copy(enc_ref.at[:, span], enc_out.at[:, span], sems.at[k]))
            copies[k].start()
        act_copy.wait()
        act = act_buf[...].T
        act_out[...] = act
        for copy, span, out in zip(copies, spans, (send_ref, keep_ref)):
            copy.wait()
            out[...] = dot(act, enc_out[:, span], ((1,), (0,)))
        for copy in copies[2:]:
            copy.wait()

    act_t = pltpu.with_memory_space_constraint(act_t, pltpu.HBM)
    encoder = pltpu.with_memory_space_constraint(encoder, pltpu.HBM)
    return call(
        body, "preact_far", (act_t, encoder), [ANYWHERE] * 2,
        [((TOK, CHUNK), F32)] * 2 + [((TOK, COL), BF16), ((COL, LAT), BF16)],
        scratch=[pltpu.VMEM((COL, TOK), BF16), pltpu.SemaphoreType.DMA, pltpu.SemaphoreType.DMA((8,))],
        flops=2_400_000_000, moved=4 * COL * CHUNK + 8 * TOK * CHUNK,
    )


def back_far(errors, dec_t):
    def body(errors_ref, dec_ref, send_ref, keep_ref):
        x, core = place()
        value = errors_ref[:, :COL]
        send_ref[...] = dot(value, dec_ref[:, columns(owner(x + FAR, 1 - core))], ((1,), (0,))).astype(BF16)
        keep_ref[...] = dot(value, dec_ref[:, columns(owner(x + FAR, core))], ((1,), (0,)))

    return call(
        body, "back_far", (errors, dec_t), [IN_VMEM] * 2, [((TOK, CHUNK), BF16), ((TOK, CHUNK), F32)],
        flops=4 * TOK * COL * CHUNK, moved=4 * COL * CHUNK + 6 * TOK * CHUNK,
    )


def rest_parts(left, right, swap, kind, name):
    def body(left_ref, right_ref, out):
        x, core = place()
        side = 1 - core if swap else core
        value = left_ref[:, :COL]
        for k, d in enumerate(REST):
            part = dot(value, right_ref[:, columns(owner(x + d, side))], ((1,), (0,)))
            out[k * TOK:(k + 1) * TOK] = part.astype(kind)

    return call(
        body, name, (left, right), [IN_VMEM] * 2, [((3 * TOK, CHUNK), kind)],
        flops=6 * TOK * COL * CHUNK, moved=6 * COL * CHUNK + 6 * TOK * CHUNK,
    )[0]


def rows_of(d):
    first = 0 if d == FAR else REST.index(d) * TOK
    return slice(first, first + TOK)


def square_sums(dec_t):
    def body(dec_ref, out_ref):
        for chunk in range(8):
            span = slice(chunk * CHUNK, chunk * CHUNK + CHUNK)
            total = jnp.sum(jnp.square(dec_ref[:, span].astype(F32)), axis=0, keepdims=True)
            out_ref[:, span] = jnp.broadcast_to(total, (8, CHUNK))

    return call(body, "square_sums", (dec_t,), [IN_VMEM], [((8, LAT), F32)], flops=2 * COL * LAT, moved=2 * COL * LAT)[0]


def pieces(value, count):
    found = []
    for _ in range(count):
        piece = value.astype(BF16).astype(F32)
        found.append(piece)
        value = value - piece
    return found


def stack_rows(rows):
    index = lax.broadcasted_iota(jnp.int32, (16, rows[0].shape[1]), 0)
    out = jnp.zeros(index.shape, F32)
    for k, row in enumerate(rows):
        out = jnp.where(index == k, row, out)
    return out.astype(BF16)


def encode(mine, other, squares, d):
    def body(mine_ref, other_ref, square_ref, square_other_ref, out_ref):
        x, core = place()
        span = columns(owner(x + d, core))
        value = mine_ref[rows_of(d)] + other_ref[rows_of(d)]
        size = jnp.abs(value)
        largest = jnp.maximum(jnp.max(size, axis=1, keepdims=True), 1e-36) * (1.0 + 2.0 ** -7)
        largest = largest.astype(BF16).astype(F32)
        power = jnp.exp2(size * (SPAN / largest) - LOWEST)
        out_ref[:TOK] = jnp.where(value == 0, 0.0, jnp.where(value < 0, -power, power)).astype(BF16)
        scale = jnp.broadcast_to(largest, (TOK, 128)).T[:1]
        out_ref[TOK:] = stack_rows([scale] + pieces(square_ref[:1, span] + square_other_ref[:1, span], 3))

    return call(
        body, "encode_sums", (mine, other, *squares), [IN_VMEM] * 4, [((ROWS, CHUNK), BF16)], moved=6 * TOK * CHUNK
    )[0]


def decode(ref):
    scale = jnp.broadcast_to(ref[TOK:TOK + 1].astype(F32), (128, TOK)).T[:, :1]
    power = ref[:TOK].astype(F32)
    size = (jnp.log(jnp.maximum(jnp.abs(power), 2e-38)) * (1.0 / LN2) + LOWEST) * (scale * (1.0 / SPAN))
    rows = ref[TOK:].astype(F32)
    return jnp.where(power == 0, 0.0, jnp.where(power < 0, -size, size)), rows[1:2] + rows[2:3] + rows[3:4]


def own_features(mine, other, parts, squares, latent_bias):
    def body(mine_ref, other_ref, *refs):
        part_refs, (square_ref, square_other_ref, bias_ref, out_ref, weight_ref) = refs[:3], refs[3:]
        x, core = place()
        span = columns(owner(x, core))
        preact = mine_ref[rows_of(0)] + other_ref[rows_of(0)] + bias_ref[:, span]
        sources = [square_ref[:1, span] + square_other_ref[:1, span]]
        for ref in part_refs:
            value, square = decode(ref)
            preact += value
            sources.append(square)
        sums = [jnp.zeros((1, CHUNK), F32) for _ in range(LAYERS)]
        for d, square in zip((0, *HOPS), sources):
            layer = lax.rem(x - d + 4, 4) // 2
            sums = [have + jnp.where(layer == k, square, 0.0) for k, have in enumerate(sums)]
        norms = [jnp.sqrt(have + EPSILON) for have in sums]
        weight_ref[...] = jnp.broadcast_to(norms[0] + norms[1], (8, CHUNK))
        out_ref[:TOK] = jnp.maximum(preact, 0.0).astype(BF16)
        out_ref[TOK:] = stack_rows(pieces(norms[0], 3) + pieces(norms[1], 3))

    return call(
        body, "own_features", (mine, other, *parts, *squares, latent_bias), [IN_VMEM] * 8,
        [((ROWS, CHUNK), BF16), ((8, CHUNK), F32)], moved=16 * TOK * CHUNK,
    )


def rebuild_first(chunks, dec_t, own_weights):
    def body(*refs):
        feats, (dec_ref, weight_ref, out_ref) = refs[:FIRST_REBUILD], refs[FIRST_REBUILD:]
        acc = jnp.zeros((TOK, COL), F32)
        for feat, chunk in zip(feats, gathered_owners()):
            acc += dot(feat[:TOK], dec_ref[:, columns(chunk)], ((1,), (1,)))
        penalty = jnp.sum(feats[0][:TOK].astype(F32) * weight_ref[:1], axis=1, keepdims=True)
        out_ref[:, :COL] = acc
        out_ref[:, COL:] = jnp.broadcast_to(penalty, (TOK, WIDE - COL))

    return call(
        body, "rebuild_first", (*chunks, dec_t, own_weights), [IN_VMEM] * (FIRST_REBUILD + 2), [((TOK, WIDE), F32)],
        flops=2 * TOK * COL * CHUNK * FIRST_REBUILD, moved=2 * COL * LAT + 2 * TOK * LAT,
    )[0]


def rebuild_last(chunks, dec_t, partial):
    def body(*refs):
        feats, (dec_ref, partial_ref, out_ref) = refs[:8 - FIRST_REBUILD], refs[8 - FIRST_REBUILD:]
        acc = partial_ref[:, :COL]
        for feat, chunk in zip(feats, gathered_owners()[FIRST_REBUILD:]):
            acc += dot(feat[:TOK], dec_ref[:, columns(chunk)], ((1,), (1,)))
        out_ref[:, :COL] = acc.astype(BF16)
        out_ref[:, COL:] = partial_ref[:, COL:].astype(BF16)

    return call(
        body, "rebuild_last", (*chunks, dec_t, partial), [IN_VMEM] * (10 - FIRST_REBUILD), [((TOK, WIDE), BF16)],
        flops=2 * TOK * COL * CHUNK * (8 - FIRST_REBUILD), moved=2 * COL * LAT + 2 * TOK * LAT,
    )[0]


def error_rows(parts, act_t, output_bias):
    def body(parts_ref, act_ref, bias_ref, out_ref):
        first = lax.axis_index("latent") * 8
        token = lax.broadcasted_iota(jnp.int32, (8, TOK), 1)
        wanted = lax.broadcasted_iota(jnp.int32, (8, TOK), 0) + first
        pick = jnp.where(token == wanted, 1.0, 0.0).astype(BF16)
        act = dot(pick, act_ref[...], ((1,), (1,)))
        total = jnp.sum(parts_ref[...].astype(F32), axis=0)
        errors = total[:, :COL] + bias_ref[...] - act
        loss = 0.5 * jnp.sum(errors * errors, axis=1, keepdims=True) + SPARSITY * total[:, COL:COL + 1]
        lane = lax.broadcasted_iota(jnp.int32, (8, WIDE - COL), 1)
        tail = jnp.zeros((8, WIDE - COL), F32)
        for k, piece in enumerate(pieces(loss, 3)):
            tail = jnp.where(lane == k, piece, tail)
        out_ref[:, :, :COL] = jnp.broadcast_to(errors.astype(BF16)[None], (32, 8, COL))
        out_ref[:, :, COL:] = jnp.broadcast_to(tail.astype(BF16)[None], (32, 8, WIDE - COL))

    return call(
        body, "error_rows", (parts, act_t, output_bias), [IN_VMEM] * 3, [((32, 8, WIDE), BF16)], moved=4 * TOK * WIDE
    )[0]


def own_gradient(mine, other, parts, features, weights, errors):
    def body(mine_ref, other_ref, one_ref, two_ref, three_ref, feat_ref, weight_ref, tail_ref, out_ref):
        total = mine_ref[rows_of(0)] + other_ref[rows_of(0)].astype(F32)
        for ref in (one_ref, two_ref, three_ref):
            total += ref[...].astype(F32)
        total += SPARSITY * weight_ref[:1]
        out_ref[:TOK] = jnp.where(feat_ref[:TOK].astype(F32) > 0, total, 0.0).astype(BF16)
        loss = jnp.sum(jnp.sum(tail_ref[:, COL:].astype(F32), axis=0, keepdims=True), axis=1, keepdims=True)
        out_ref[TOK:] = stack_rows([jnp.broadcast_to(piece, (1, CHUNK)) for piece in pieces(loss, 3)])

    return call(
        body, "own_gradient", (mine, other, *parts, features, weights, errors), [IN_VMEM] * 8,
        [((ROWS, CHUNK), BF16)], moved=16 * TOK * CHUNK,
    )[0]


def store_chunks(values, owners, out_ref, buffer, sems):
    copies = []
    for k, chunk in enumerate(owners):
        buffer[k] = values(k, chunk)
        copies.append(pltpu.make_async_copy(buffer.at[k], out_ref.at[:, columns(chunk)], sems.at[k]))
        copies[-1].start()
    for copy in copies:
        copy.wait()


def decoder_gradient(errors, chunks, dec_t):
    def body(errors_ref, *refs):
        feats, (dec_ref, out_ref, sum_ref, buffer, sems) = refs[:8], refs[8:]
        x, _ = place()
        layer = x // 2
        error = errors_ref[:, :COL].T

        def values(k, chunk):
            feat = feats[k][:TOK]
            rows = feats[k][TOK:].astype(F32)
            norm = jnp.where(layer == 0, rows[0:1] + rows[1:2] + rows[2:3], rows[3:4] + rows[4:5] + rows[5:6])
            totals = jnp.sum(feat.astype(F32), axis=0, keepdims=True)
            scale = SPARSITY * totals / norm
            return (dot(error, feat, ((1,), (0,))) + scale * dec_ref[:, columns(chunk)].astype(F32)).astype(BF16)

        store_chunks(values, gathered_owners(), out_ref, buffer, sems)
        sum_ref[...] = jnp.sum(errors_ref[:, :COL].astype(F32), axis=0, keepdims=True)

    return call(
        body, "decoder_gradient", (errors, *chunks, dec_t), [IN_VMEM] * 10,
        [((COL, LAT), BF16), ((1, COL), F32)], out_specs=[ANYWHERE, IN_VMEM],
        scratch=[pltpu.VMEM((8, COL, CHUNK), BF16), pltpu.SemaphoreType.DMA((8,))],
        flops=2 * TOK * COL * LAT, moved=4 * COL * LAT + 2 * TOK * LAT,
    )


def loss_rows(grads):
    loss = jnp.zeros((1, 128), F32)
    for grad in grads:
        rows = grad[TOK:, :128].astype(F32)
        loss += rows[0:1] + rows[1:2] + rows[2:3]
    return loss * (1.0 / (TOK * LAYERS * D))


def encoder_gradient(act_t, chunks):
    def body(act_ref, *refs):
        grads, (out_ref, sum_ref, loss_ref, buffer, sum_buf, loss_buf, sems, small_sems) = refs[:8], refs[8:]
        loss_buf[...] = loss_rows(grads)
        for grad, chunk in zip(grads, gathered_owners(BACKWARD)):
            sum_buf[:, columns(chunk)] = jnp.sum(grad[:TOK].astype(F32), axis=0, keepdims=True)
        small = [
            pltpu.make_async_copy(sum_buf, sum_ref, small_sems.at[0]),
            pltpu.make_async_copy(loss_buf, loss_ref, small_sems.at[1]),
        ]
        for copy in small:
            copy.start()
        store_chunks(
            lambda k, chunk: dot(act_ref[...], grads[k][:TOK], ((1,), (0,))).astype(BF16),
            gathered_owners(BACKWARD), out_ref, buffer, sems,
        )
        for copy in small:
            copy.wait()

    return call(
        body, "encoder_gradient", (act_t, *chunks), [IN_VMEM] * 9,
        [((COL, LAT), BF16), ((1, LAT), F32), ((1, 128), F32)], out_specs=[ANYWHERE] * 3,
        scratch=[
            pltpu.VMEM((8, COL, CHUNK), BF16), pltpu.VMEM((1, LAT), F32), pltpu.VMEM((1, 128), F32),
            pltpu.SemaphoreType.DMA((8,)), pltpu.SemaphoreType.DMA((2,)),
        ],
        flops=2 * TOK * COL * LAT, moved=2 * COL * LAT + 2 * TOK * LAT,
    )


def gather_chunks(own, hops):
    moved = [own] + [on_width(own, x_shift(d)) for d in hops]
    return [chunk for part in moved for chunk in (part, on_width(part, CORE_SWAP))]


def shards(activations, encoder, latent_bias, decoder, output_bias):
    act_t, dec_t = activations.T, decoder.T

    send, keep_far, act, enc = preact_far(act_t, encoder)
    send, early_dec = lax.optimization_barrier((send, dec_t))
    squares = square_sums(early_dec)
    squares = (squares, on_width(squares, CORE_SWAP))
    far = (keep_far, on_width(send, CORE_SWAP))
    send = rest_parts(act, enc, True, F32, "preact_send")
    keep = rest_parts(act, enc, False, F32, "preact_keep")
    coded, send, keep = lax.optimization_barrier((encode(*far, squares, FAR), send, keep))
    rest = (keep, on_width(send, CORE_SWAP))
    coded = [on_width(coded, x_shift(FAR))] + [on_width(encode(*rest, squares, d), x_shift(d)) for d in HOPS[1:]]
    features, own_weights = own_features(*rest, coded, squares, latent_bias[None, :])

    feature_chunks = gather_chunks(features, HOPS)
    partial = rebuild_first(feature_chunks[:FIRST_REBUILD], dec_t, own_weights)
    parts = rebuild_last(feature_chunks[FIRST_REBUILD:], dec_t, partial).reshape(32, 8, WIDE)
    parts, bias_row = lax.optimization_barrier((parts, output_bias[None, :]))
    parts = lax.all_to_all(parts, "latent", 0, 0)
    errors = error_rows(parts, act_t, bias_row)
    errors = lax.all_to_all(errors, "latent", 0, 0).reshape(TOK, WIDE)

    send, keep_far = back_far(errors, dec_t)
    send, keep_far, errors = lax.optimization_barrier((send, keep_far, errors))
    summed = keep_far + on_width(send, CORE_SWAP).astype(F32)
    send = rest_parts(errors, dec_t, True, BF16, "back_send")
    keep = rest_parts(errors, dec_t, False, F32, "back_keep")
    summed, send, keep = lax.optimization_barrier((summed.astype(BF16), send, keep))
    summed = [on_width(summed, x_shift(FAR))]
    rest = (keep, on_width(send, CORE_SWAP))
    for d in HOPS[1:]:
        total = rest[0][rows_of(d)] + rest[1][rows_of(d)].astype(F32)
        summed.append(on_width(total.astype(BF16), x_shift(d)))
    decoder_grad, output_grad = decoder_gradient(errors, feature_chunks, dec_t)
    decoder_grad, output_grad, features = lax.optimization_barrier((decoder_grad, output_grad[0], features))
    grad_pre = own_gradient(*rest, summed, features, own_weights, errors)
    encoder_grad, latent_grad, loss_value = encoder_gradient(act_t, gather_chunks(grad_pre, BACKWARD))
    return (loss_value[0, 0], encoder_grad, latent_grad[0], decoder_grad.T, output_grad)


def solution(mesh):
    placed = (P(None, "width"), P("width", "latent"), P("latent"), P("latent", "width"), P("width"))
    return jax.shard_map(
        shards,
        mesh=mesh,
        in_specs=placed,
        out_specs=(P(), P("width", "latent"), P("latent"), P("latent", "width"), P("width")),
        check_vma=False,
    )
```

```python
import jax
import jax.numpy as jnp
from jax import lax
from jax.experimental import pallas as pl
from jax.experimental.pallas import tpu as pltpu
from jax.sharding import PartitionSpec as P

D = 2304
LAYERS = 2
SPARSITY = 0.5
EPSILON = 1e-06
F32 = jnp.float32
BF16 = jnp.bfloat16
TOK = 256
COL = 576
CHUNK = 256
WIDE = 640
LAT = 2048
ROWS = TOK + 16
SPAN = 250.0
LOWEST = 125.0
LN2 = 0.6931471805599453
FAR = 2
HOPS = (FAR, 1, 3)
BACKWARD = HOPS[::-1]
REST = (1, 3, 0)
FIRST_REBUILD = 4
VMEM_BYTES = 16 * 1024 * 1024

CORE_SWAP = [(i, i ^ 1) for i in range(8)]


def x_shift(d):
    return [(i, (i + 2 * d) % 8) for i in range(8)]


def on_width(value, pairs):
    return lax.ppermute(value, "width", pairs)


def dot(a, b, dims):
    return lax.dot_general(a, b, (dims, ((), ())), preferred_element_type=F32)


IN_VMEM = pl.BlockSpec(memory_space=pltpu.VMEM)
ANYWHERE = pl.BlockSpec(memory_space=pl.ANY)


def call(body, name, args, in_specs, outs, out_specs=None, scratch=(), flops=0, moved=0):
    return pl.pallas_call(
        body,
        in_specs=in_specs,
        out_specs=out_specs or [IN_VMEM] * len(outs),
        out_shape=[jax.ShapeDtypeStruct(shape, kind) for shape, kind in outs],
        scratch_shapes=list(scratch),
        compiler_params=pltpu.CompilerParams(vmem_limit_bytes=VMEM_BYTES),
        name=name,
        cost_estimate=pl.CostEstimate(flops=flops, bytes_accessed=moved, transcendentals=0),
    )(*args)


def place():
    width_index = lax.axis_index("width")
    return width_index // 2, width_index % 2


def owner(x, core):
    return lax.rem(x + 4, 4) * 2 + core


def gathered_owners(hops=HOPS):
    x, core = place()
    return [owner(x - d, side) for d in (0, *hops) for side in (core, 1 - core)]


def columns(chunk):
    return pl.ds(pl.multiple_of(chunk * CHUNK, CHUNK), CHUNK)


def preact_far(act_t, encoder):
    def body(act_ref, enc_ref, send_ref, keep_ref, act_out, enc_out, act_buf, act_sem, sems):
        x, core = place()
        act_copy = pltpu.make_async_copy(act_ref, act_buf, act_sem)
        act_copy.start()
        spans = [columns(owner(x + d, side)) for d in (FAR, *REST) for side in (1 - core, core)]
        copies = []
        for k, span in enumerate(spans):
            copies.append(pltpu.make_async_copy(enc_ref.at[:, span], enc_out.at[:, span], sems.at[k]))
            copies[k].start()
        act_copy.wait()
        act = act_buf[...].T
        act_out[...] = act
        for copy, span, out in zip(copies, spans, (send_ref, keep_ref)):
            copy.wait()
            out[...] = dot(act, enc_out[:, span], ((1,), (0,)))
        for copy in copies[2:]:
            copy.wait()

    act_t = pltpu.with_memory_space_constraint(act_t, pltpu.HBM)
    encoder = pltpu.with_memory_space_constraint(encoder, pltpu.HBM)
    return call(
        body, "preact_far", (act_t, encoder), [ANYWHERE] * 2,
        [((TOK, CHUNK), F32)] * 2 + [((TOK, COL), BF16), ((COL, LAT), BF16)],
        scratch=[pltpu.VMEM((COL, TOK), BF16), pltpu.SemaphoreType.DMA, pltpu.SemaphoreType.DMA((8,))],
        flops=2_400_000_000, moved=4 * COL * CHUNK + 8 * TOK * CHUNK,
    )


def back_far(errors, dec_t):
    def body(errors_ref, dec_ref, send_ref):
        x, core = place()
        span = columns(owner(x + FAR, 1 - core))
        send_ref[...] = dot(errors_ref[:, :COL], dec_ref[:, span], ((1,), (0,))).astype(BF16)

    return call(
        body, "back_far", (errors, dec_t), [IN_VMEM] * 2, [((TOK, CHUNK), BF16)],
        flops=2 * TOK * COL * CHUNK, moved=2 * COL * CHUNK + 2 * TOK * CHUNK,
    )[0]


def back_keep(errors, dec_t):
    def body(errors_ref, dec_ref, far_ref, out_ref):
        x, core = place()
        value = errors_ref[:, :COL]
        far_ref[...] = dot(value, dec_ref[:, columns(owner(x + FAR, core))], ((1,), (0,)))
        for k, d in enumerate(REST):
            part = dot(value, dec_ref[:, columns(owner(x + d, core))], ((1,), (0,)))
            out_ref[k * TOK:(k + 1) * TOK] = part

    return call(
        body, "back_keep", (errors, dec_t), [IN_VMEM] * 2, [((TOK, CHUNK), F32), ((3 * TOK, CHUNK), F32)],
        flops=8 * TOK * COL * CHUNK, moved=8 * COL * CHUNK + 16 * TOK * CHUNK,
    )


def rest_parts(left, right, swap, kind, name):
    def body(left_ref, right_ref, out):
        x, core = place()
        side = 1 - core if swap else core
        value = left_ref[:, :COL]
        for k, d in enumerate(REST):
            part = dot(value, right_ref[:, columns(owner(x + d, side))], ((1,), (0,)))
            out[k * TOK:(k + 1) * TOK] = part.astype(kind)

    return call(
        body, name, (left, right), [IN_VMEM] * 2, [((3 * TOK, CHUNK), kind)],
        flops=6 * TOK * COL * CHUNK, moved=6 * COL * CHUNK + 6 * TOK * CHUNK,
    )[0]


def rows_of(d):
    first = 0 if d == FAR else REST.index(d) * TOK
    return slice(first, first + TOK)


def square_sums(dec_t):
    def body(dec_ref, out_ref):
        for chunk in range(8):
            span = slice(chunk * CHUNK, chunk * CHUNK + CHUNK)
            total = jnp.sum(jnp.square(dec_ref[:, span].astype(F32)), axis=0, keepdims=True)
            out_ref[:, span] = jnp.broadcast_to(total, (8, CHUNK))

    return call(body, "square_sums", (dec_t,), [IN_VMEM], [((8, LAT), F32)], flops=2 * COL * LAT, moved=2 * COL * LAT)[0]


def pieces(value, count):
    found = []
    for _ in range(count):
        piece = value.astype(BF16).astype(F32)
        found.append(piece)
        value = value - piece
    return found


def stack_rows(rows):
    index = lax.broadcasted_iota(jnp.int32, (16, rows[0].shape[1]), 0)
    out = jnp.zeros(index.shape, F32)
    for k, row in enumerate(rows):
        out = jnp.where(index == k, row, out)
    return out.astype(BF16)


def encode(mine, other, squares, d):
    def body(mine_ref, other_ref, square_ref, square_other_ref, out_ref):
        x, core = place()
        span = columns(owner(x + d, core))
        value = mine_ref[rows_of(d)] + other_ref[rows_of(d)]
        size = jnp.abs(value)
        largest = jnp.maximum(jnp.max(size, axis=1, keepdims=True), 1e-36) * (1.0 + 2.0 ** -7)
        largest = largest.astype(BF16).astype(F32)
        power = jnp.exp2(size * (SPAN / largest) - LOWEST)
        out_ref[:TOK] = jnp.where(value == 0, 0.0, jnp.where(value < 0, -power, power)).astype(BF16)
        scale = jnp.broadcast_to(largest, (TOK, 128)).T[:1]
        out_ref[TOK:] = stack_rows([scale] + pieces(square_ref[:1, span] + square_other_ref[:1, span], 3))

    return call(
        body, "encode_sums", (mine, other, *squares), [IN_VMEM] * 4, [((ROWS, CHUNK), BF16)], moved=6 * TOK * CHUNK
    )[0]


def decode(ref):
    scale = jnp.broadcast_to(ref[TOK:TOK + 1].astype(F32), (128, TOK)).T[:, :1]
    power = ref[:TOK].astype(F32)
    size = (jnp.log(jnp.maximum(jnp.abs(power), 2e-38)) * (1.0 / LN2) + LOWEST) * (scale * (1.0 / SPAN))
    rows = ref[TOK:].astype(F32)
    return jnp.where(power == 0, 0.0, jnp.where(power < 0, -size, size)), rows[1:2] + rows[2:3] + rows[3:4]


def own_features(mine, other, parts, squares, latent_bias):
    def body(mine_ref, other_ref, *refs):
        part_refs, (square_ref, square_other_ref, bias_ref, out_ref, weight_ref) = refs[:3], refs[3:]
        x, core = place()
        span = columns(owner(x, core))
        preact = mine_ref[rows_of(0)] + other_ref[rows_of(0)] + bias_ref[:, span]
        sources = [square_ref[:1, span] + square_other_ref[:1, span]]
        for ref in part_refs:
            value, square = decode(ref)
            preact += value
            sources.append(square)
        sums = [jnp.zeros((1, CHUNK), F32) for _ in range(LAYERS)]
        for d, square in zip((0, *HOPS), sources):
            layer = lax.rem(x - d + 4, 4) // 2
            sums = [have + jnp.where(layer == k, square, 0.0) for k, have in enumerate(sums)]
        norms = [jnp.sqrt(have + EPSILON) for have in sums]
        weight_ref[...] = jnp.broadcast_to(norms[0] + norms[1], (8, CHUNK))
        out_ref[:TOK] = jnp.maximum(preact, 0.0).astype(BF16)
        out_ref[TOK:] = stack_rows(pieces(norms[0], 3) + pieces(norms[1], 3))

    return call(
        body, "own_features", (mine, other, *parts, *squares, latent_bias), [IN_VMEM] * 8,
        [((ROWS, CHUNK), BF16), ((8, CHUNK), F32)], moved=16 * TOK * CHUNK,
    )


def rebuild_first(chunks, dec_t, own_weights):
    def body(*refs):
        feats, (dec_ref, weight_ref, out_ref) = refs[:FIRST_REBUILD], refs[FIRST_REBUILD:]
        acc = jnp.zeros((TOK, COL), F32)
        for feat, chunk in zip(feats, gathered_owners()):
            acc += dot(feat[:TOK], dec_ref[:, columns(chunk)], ((1,), (1,)))
        penalty = jnp.sum(feats[0][:TOK].astype(F32) * weight_ref[:1], axis=1, keepdims=True)
        out_ref[:, :COL] = acc
        out_ref[:, COL:] = jnp.broadcast_to(penalty, (TOK, WIDE - COL))

    return call(
        body, "rebuild_first", (*chunks, dec_t, own_weights), [IN_VMEM] * (FIRST_REBUILD + 2), [((TOK, WIDE), F32)],
        flops=2 * TOK * COL * CHUNK * FIRST_REBUILD, moved=2 * COL * LAT + 2 * TOK * LAT,
    )[0]


def rebuild_last(chunks, dec_t, partial):
    def body(*refs):
        feats, (dec_ref, partial_ref, out_ref) = refs[:8 - FIRST_REBUILD], refs[8 - FIRST_REBUILD:]
        acc = partial_ref[:, :COL]
        for feat, chunk in zip(feats, gathered_owners()[FIRST_REBUILD:]):
            acc += dot(feat[:TOK], dec_ref[:, columns(chunk)], ((1,), (1,)))
        out_ref[:, :COL] = acc.astype(BF16)
        out_ref[:, COL:] = partial_ref[:, COL:].astype(BF16)

    return call(
        body, "rebuild_last", (*chunks, dec_t, partial), [IN_VMEM] * (10 - FIRST_REBUILD), [((TOK, WIDE), BF16)],
        flops=2 * TOK * COL * CHUNK * (8 - FIRST_REBUILD), moved=2 * COL * LAT + 2 * TOK * LAT,
    )[0]


def offset_rows(act_t, output_bias):
    def body(act_ref, bias_ref, out_ref):
        first = lax.axis_index("latent") * 8
        token = lax.broadcasted_iota(jnp.int32, (8, TOK), 1)
        wanted = lax.broadcasted_iota(jnp.int32, (8, TOK), 0) + first
        pick = jnp.where(token == wanted, 1.0, 0.0).astype(BF16)
        out_ref[...] = bias_ref[...] - dot(pick, act_ref[...], ((1,), (1,)))

    return call(body, "offset_rows", (act_t, output_bias), [IN_VMEM] * 2, [((8, COL), F32)], moved=2 * TOK * COL)[0]


def error_rows(parts, offset):
    def body(parts_ref, offset_ref, out_ref):
        total = jnp.sum(parts_ref[...].astype(F32), axis=0)
        errors = total[:, :COL] + offset_ref[...]
        loss = 0.5 * jnp.sum(errors * errors, axis=1, keepdims=True) + SPARSITY * total[:, COL:COL + 1]
        lane = lax.broadcasted_iota(jnp.int32, (8, WIDE - COL), 1)
        tail = jnp.zeros((8, WIDE - COL), F32)
        for k, piece in enumerate(pieces(loss, 3)):
            tail = jnp.where(lane == k, piece, tail)
        out_ref[:, :, :COL] = jnp.broadcast_to(errors.astype(BF16)[None], (32, 8, COL))
        out_ref[:, :, COL:] = jnp.broadcast_to(tail.astype(BF16)[None], (32, 8, WIDE - COL))

    return call(
        body, "error_rows", (parts, offset), [IN_VMEM] * 2, [((32, 8, WIDE), BF16)], moved=4 * TOK * WIDE
    )[0]


def own_gradient(mine, other, parts, features, weights, errors):
    def body(mine_ref, other_ref, one_ref, two_ref, three_ref, feat_ref, weight_ref, tail_ref, out_ref):
        total = mine_ref[rows_of(0)] + other_ref[rows_of(0)].astype(F32)
        for ref in (one_ref, two_ref, three_ref):
            total += ref[...].astype(F32)
        total += SPARSITY * weight_ref[:1]
        out_ref[:TOK] = jnp.where(feat_ref[:TOK].astype(F32) > 0, total, 0.0).astype(BF16)
        loss = jnp.sum(jnp.sum(tail_ref[:, COL:].astype(F32), axis=0, keepdims=True), axis=1, keepdims=True)
        out_ref[TOK:] = stack_rows([jnp.broadcast_to(piece, (1, CHUNK)) for piece in pieces(loss, 3)])

    return call(
        body, "own_gradient", (mine, other, *parts, features, weights, errors), [IN_VMEM] * 8,
        [((ROWS, CHUNK), BF16)], moved=16 * TOK * CHUNK,
    )[0]


def store_chunks(values, owners, out_ref, buffer, sems):
    copies = []
    for k, chunk in enumerate(owners):
        buffer[k] = values(k, chunk)
        copies.append(pltpu.make_async_copy(buffer.at[k], out_ref.at[:, columns(chunk)], sems.at[k]))
        copies[-1].start()
    for copy in copies:
        copy.wait()


def decoder_gradient(errors, chunks, dec_t):
    def body(errors_ref, *refs):
        feats, (dec_ref, out_ref, sum_ref, buffer, sems) = refs[:8], refs[8:]
        x, _ = place()
        layer = x // 2
        error = errors_ref[:, :COL].T

        def values(k, chunk):
            feat = feats[k][:TOK]
            rows = feats[k][TOK:].astype(F32)
            norm = jnp.where(layer == 0, rows[0:1] + rows[1:2] + rows[2:3], rows[3:4] + rows[4:5] + rows[5:6])
            totals = jnp.sum(feat.astype(F32), axis=0, keepdims=True)
            scale = SPARSITY * totals / norm
            return (dot(error, feat, ((1,), (0,))) + scale * dec_ref[:, columns(chunk)].astype(F32)).astype(BF16)

        store_chunks(values, gathered_owners(), out_ref, buffer, sems)
        sum_ref[...] = jnp.sum(errors_ref[:, :COL].astype(F32), axis=0, keepdims=True)

    return call(
        body, "decoder_gradient", (errors, *chunks, dec_t), [IN_VMEM] * 10,
        [((COL, LAT), BF16), ((1, COL), F32)], out_specs=[ANYWHERE, IN_VMEM],
        scratch=[pltpu.VMEM((8, COL, CHUNK), BF16), pltpu.SemaphoreType.DMA((8,))],
        flops=2 * TOK * COL * LAT, moved=4 * COL * LAT + 2 * TOK * LAT,
    )


def loss_rows(grads):
    loss = jnp.zeros((1, 128), F32)
    for grad in grads:
        rows = grad[TOK:, :128].astype(F32)
        loss += rows[0:1] + rows[1:2] + rows[2:3]
    return loss * (1.0 / (TOK * LAYERS * D))


def encoder_gradient(act_t, chunks):
    def body(act_ref, *refs):
        grads, (out_ref, sum_ref, loss_ref, buffer, sum_buf, loss_buf, sems, small_sems) = refs[:8], refs[8:]
        loss_buf[...] = loss_rows(grads)
        for grad, chunk in zip(grads, gathered_owners(BACKWARD)):
            sum_buf[:, columns(chunk)] = jnp.sum(grad[:TOK].astype(F32), axis=0, keepdims=True)
        small = [
            pltpu.make_async_copy(sum_buf, sum_ref, small_sems.at[0]),
            pltpu.make_async_copy(loss_buf, loss_ref, small_sems.at[1]),
        ]
        for copy in small:
            copy.start()
        store_chunks(
            lambda k, chunk: dot(act_ref[...], grads[k][:TOK], ((1,), (0,))).astype(BF16),
            gathered_owners(BACKWARD), out_ref, buffer, sems,
        )
        for copy in small:
            copy.wait()

    return call(
        body, "encoder_gradient", (act_t, *chunks), [IN_VMEM] * 9,
        [((COL, LAT), BF16), ((1, LAT), F32), ((1, 128), F32)], out_specs=[ANYWHERE] * 3,
        scratch=[
            pltpu.VMEM((8, COL, CHUNK), BF16), pltpu.VMEM((1, LAT), F32), pltpu.VMEM((1, 128), F32),
            pltpu.SemaphoreType.DMA((8,)), pltpu.SemaphoreType.DMA((2,)),
        ],
        flops=2 * TOK * COL * LAT, moved=2 * COL * LAT + 2 * TOK * LAT,
    )


def gather_chunks(own, hops):
    moved = [own] + [on_width(own, x_shift(d)) for d in hops]
    return [chunk for part in moved for chunk in (part, on_width(part, CORE_SWAP))]


def shards(activations, encoder, latent_bias, decoder, output_bias):
    act_t, dec_t = activations.T, decoder.T

    send, keep_far, act, enc = preact_far(act_t, encoder)
    send, early_dec = lax.optimization_barrier((send, dec_t))
    squares = square_sums(early_dec)
    squares = (squares, on_width(squares, CORE_SWAP))
    far = (keep_far, on_width(send, CORE_SWAP))
    send = rest_parts(act, enc, True, F32, "preact_send")
    keep = rest_parts(act, enc, False, F32, "preact_keep")
    coded, send, keep = lax.optimization_barrier((encode(*far, squares, FAR), send, keep))
    rest = (keep, on_width(send, CORE_SWAP))
    coded = [on_width(coded, x_shift(FAR))] + [on_width(encode(*rest, squares, d), x_shift(d)) for d in HOPS[1:]]
    features, own_weights = own_features(*rest, coded, squares, latent_bias[None, :])

    feature_chunks = gather_chunks(features, HOPS)
    partial = rebuild_first(feature_chunks[:FIRST_REBUILD], dec_t, own_weights)
    parts = rebuild_last(feature_chunks[FIRST_REBUILD:], dec_t, partial).reshape(32, 8, WIDE)
    parts, offset = lax.optimization_barrier((parts, offset_rows(act_t, output_bias[None, :])))
    parts = lax.all_to_all(parts, "latent", 0, 0)
    errors = error_rows(parts, offset)
    errors = lax.all_to_all(errors, "latent", 0, 0).reshape(TOK, WIDE)

    send = back_far(errors, dec_t)
    send, errors = lax.optimization_barrier((send, errors))
    keep_far, keep = back_keep(errors, dec_t)
    summed = keep_far + on_width(send, CORE_SWAP).astype(F32)
    send = rest_parts(errors, dec_t, True, BF16, "back_send")
    summed, send, keep = lax.optimization_barrier((summed.astype(BF16), send, keep))
    summed = [on_width(summed, x_shift(FAR))]
    rest = (keep, on_width(send, CORE_SWAP))
    for d in HOPS[1:]:
        total = rest[0][rows_of(d)] + rest[1][rows_of(d)].astype(F32)
        summed.append(on_width(total.astype(BF16), x_shift(d)))
    decoder_grad, output_grad = decoder_gradient(errors, feature_chunks, dec_t)
    decoder_grad, output_grad, features = lax.optimization_barrier((decoder_grad, output_grad[0], features))
    grad_pre = own_gradient(*rest, summed, features, own_weights, errors)
    encoder_grad, latent_grad, loss_value = encoder_gradient(act_t, gather_chunks(grad_pre, BACKWARD))
    return (loss_value[0, 0], encoder_grad, latent_grad[0], decoder_grad.T, output_grad)


def solution(mesh):
    placed = (P(None, "width"), P("width", "latent"), P("latent"), P("latent", "width"), P("width"))
    return jax.shard_map(
        shards,
        mesh=mesh,
        in_specs=placed,
        out_specs=(P(), P("width", "latent"), P("latent"), P("latent", "width"), P("width")),
        check_vma=False,
    )
```

```python
import jax
import jax.numpy as jnp
from jax import lax
from jax.experimental import pallas as pl
from jax.experimental.pallas import tpu as pltpu
from jax.sharding import PartitionSpec as P

D = 2304
LAYERS = 2
SPARSITY = 0.5
EPSILON = 1e-06
F32 = jnp.float32
BF16 = jnp.bfloat16
TOK = 256
COL = 576
CHUNK = 256
WIDE = 640
LAT = 2048
ROWS = TOK + 16
SPAN = 250.0
LOWEST = 125.0
LN2 = 0.6931471805599453
FAR = 2
HOPS = (FAR, 1, 3)
FORWARD = (3, FAR, 1)
BACKWARD = HOPS[::-1]
REST = (1, 3, 0)
FIRST_REBUILD = 6
VMEM_BYTES = 16 * 1024 * 1024

CORE_SWAP = [(i, i ^ 1) for i in range(8)]


def x_shift(d):
    return [(i, (i + 2 * d) % 8) for i in range(8)]


def on_width(value, pairs):
    return lax.ppermute(value, "width", pairs)


def dot(a, b, dims):
    return lax.dot_general(a, b, (dims, ((), ())), preferred_element_type=F32)


IN_VMEM = pl.BlockSpec(memory_space=pltpu.VMEM)
ANYWHERE = pl.BlockSpec(memory_space=pl.ANY)


def call(body, name, args, in_specs, outs, out_specs=None, scratch=(), flops=0, moved=0):
    return pl.pallas_call(
        body,
        in_specs=in_specs,
        out_specs=out_specs or [IN_VMEM] * len(outs),
        out_shape=[jax.ShapeDtypeStruct(shape, kind) for shape, kind in outs],
        scratch_shapes=list(scratch),
        compiler_params=pltpu.CompilerParams(vmem_limit_bytes=VMEM_BYTES),
        name=name,
        cost_estimate=pl.CostEstimate(flops=flops, bytes_accessed=moved, transcendentals=0),
    )(*args)


def place():
    width_index = lax.axis_index("width")
    return width_index // 2, width_index % 2


def owner(x, core):
    return lax.rem(x + 4, 4) * 2 + core


def gathered_owners(hops=FORWARD):
    x, core = place()
    return [owner(x - d, side) for d in (0, *hops) for side in (core, 1 - core)]


def columns(chunk):
    return pl.ds(pl.multiple_of(chunk * CHUNK, CHUNK), CHUNK)


def preact_far(act_t, encoder):
    def body(act_ref, enc_ref, send_ref, keep_ref, act_out, enc_out, act_buf, act_sem, sems):
        x, core = place()
        act_copy = pltpu.make_async_copy(act_ref, act_buf, act_sem)
        act_copy.start()
        spans = [columns(owner(x + d, side)) for d in (FAR, *REST) for side in (1 - core, core)]
        copies = []
        for k, span in enumerate(spans):
            copies.append(pltpu.make_async_copy(enc_ref.at[:, span], enc_out.at[:, span], sems.at[k]))
            copies[k].start()
        act_copy.wait()
        act = act_buf[...].T
        act_out[...] = act
        for copy, span, out in zip(copies, spans, (send_ref, keep_ref)):
            copy.wait()
            out[...] = dot(act, enc_out[:, span], ((1,), (0,)))
        for copy in copies[2:]:
            copy.wait()

    act_t = pltpu.with_memory_space_constraint(act_t, pltpu.HBM)
    encoder = pltpu.with_memory_space_constraint(encoder, pltpu.HBM)
    return call(
        body, "preact_far", (act_t, encoder), [ANYWHERE] * 2,
        [((TOK, CHUNK), F32)] * 2 + [((TOK, COL), BF16), ((COL, LAT), BF16)],
        scratch=[pltpu.VMEM((COL, TOK), BF16), pltpu.SemaphoreType.DMA, pltpu.SemaphoreType.DMA((8,))],
        flops=2_400_000_000, moved=4 * COL * CHUNK + 8 * TOK * CHUNK,
    )


def back_far(errors, dec_t):
    def body(errors_ref, dec_ref, send_ref):
        x, core = place()
        span = columns(owner(x + FAR, 1 - core))
        send_ref[...] = dot(errors_ref[:, :COL], dec_ref[:, span], ((1,), (0,))).astype(BF16)

    return call(
        body, "back_far", (errors, dec_t), [IN_VMEM] * 2, [((TOK, CHUNK), BF16)],
        flops=2 * TOK * COL * CHUNK, moved=2 * COL * CHUNK + 2 * TOK * CHUNK,
    )[0]


def back_keep(errors, dec_t):
    def body(errors_ref, dec_ref, far_ref, out_ref):
        x, core = place()
        value = errors_ref[:, :COL]
        far_ref[...] = dot(value, dec_ref[:, columns(owner(x + FAR, core))], ((1,), (0,)))
        for k, d in enumerate(REST):
            part = dot(value, dec_ref[:, columns(owner(x + d, core))], ((1,), (0,)))
            out_ref[k * TOK:(k + 1) * TOK] = part

    return call(
        body, "back_keep", (errors, dec_t), [IN_VMEM] * 2, [((TOK, CHUNK), F32), ((3 * TOK, CHUNK), F32)],
        flops=8 * TOK * COL * CHUNK, moved=8 * COL * CHUNK + 16 * TOK * CHUNK,
    )


def rest_parts(left, right, swap, kind, name):
    def body(left_ref, right_ref, out):
        x, core = place()
        side = 1 - core if swap else core
        value = left_ref[:, :COL]
        for k, d in enumerate(REST):
            part = dot(value, right_ref[:, columns(owner(x + d, side))], ((1,), (0,)))
            out[k * TOK:(k + 1) * TOK] = part.astype(kind)

    return call(
        body, name, (left, right), [IN_VMEM] * 2, [((3 * TOK, CHUNK), kind)],
        flops=6 * TOK * COL * CHUNK, moved=6 * COL * CHUNK + 6 * TOK * CHUNK,
    )[0]


def rows_of(d):
    first = 0 if d == FAR else REST.index(d) * TOK
    return slice(first, first + TOK)


def square_sums(dec_t):
    def body(dec_ref, out_ref):
        for chunk in range(8):
            span = slice(chunk * CHUNK, chunk * CHUNK + CHUNK)
            total = jnp.sum(jnp.square(dec_ref[:, span].astype(F32)), axis=0, keepdims=True)
            out_ref[:, span] = jnp.broadcast_to(total, (8, CHUNK))

    return call(body, "square_sums", (dec_t,), [IN_VMEM], [((8, LAT), F32)], flops=2 * COL * LAT, moved=2 * COL * LAT)[0]


def pieces(value, count):
    found = []
    for _ in range(count):
        piece = value.astype(BF16).astype(F32)
        found.append(piece)
        value = value - piece
    return found


def stack_rows(rows):
    index = lax.broadcasted_iota(jnp.int32, (16, rows[0].shape[1]), 0)
    out = jnp.zeros(index.shape, F32)
    for k, row in enumerate(rows):
        out = jnp.where(index == k, row, out)
    return out.astype(BF16)


def encode(mine, other, squares, d):
    def body(mine_ref, other_ref, square_ref, square_other_ref, out_ref):
        x, core = place()
        span = columns(owner(x + d, core))
        value = mine_ref[rows_of(d)] + other_ref[rows_of(d)]
        size = jnp.abs(value)
        largest = jnp.maximum(jnp.max(size, axis=1, keepdims=True), 1e-36) * (1.0 + 2.0 ** -7)
        largest = largest.astype(BF16).astype(F32)
        power = jnp.exp2(size * (SPAN / largest) - LOWEST)
        out_ref[:TOK] = jnp.where(value == 0, 0.0, jnp.where(value < 0, -power, power)).astype(BF16)
        scale = jnp.broadcast_to(largest, (TOK, 128)).T[:1]
        out_ref[TOK:] = stack_rows([scale] + pieces(square_ref[:1, span] + square_other_ref[:1, span], 3))

    return call(
        body, "encode_sums", (mine, other, *squares), [IN_VMEM] * 4, [((ROWS, CHUNK), BF16)], moved=6 * TOK * CHUNK
    )[0]


def decode(ref):
    scale = jnp.broadcast_to(ref[TOK:TOK + 1].astype(F32), (128, TOK)).T[:, :1]
    power = ref[:TOK].astype(F32)
    size = (jnp.log(jnp.maximum(jnp.abs(power), 2e-38)) * (1.0 / LN2) + LOWEST) * (scale * (1.0 / SPAN))
    rows = ref[TOK:].astype(F32)
    return jnp.where(power == 0, 0.0, jnp.where(power < 0, -size, size)), rows[1:2] + rows[2:3] + rows[3:4]


def own_features(mine, other, parts, squares, latent_bias):
    def body(mine_ref, other_ref, *refs):
        part_refs, (square_ref, square_other_ref, bias_ref, out_ref, weight_ref) = refs[:3], refs[3:]
        x, core = place()
        span = columns(owner(x, core))
        preact = mine_ref[rows_of(0)] + other_ref[rows_of(0)] + bias_ref[:, span]
        sources = [square_ref[:1, span] + square_other_ref[:1, span]]
        for ref in part_refs:
            value, square = decode(ref)
            preact += value
            sources.append(square)
        sums = [jnp.zeros((1, CHUNK), F32) for _ in range(LAYERS)]
        for d, square in zip((0, *HOPS), sources):
            layer = lax.rem(x - d + 4, 4) // 2
            sums = [have + jnp.where(layer == k, square, 0.0) for k, have in enumerate(sums)]
        norms = [jnp.sqrt(have + EPSILON) for have in sums]
        weight_ref[...] = jnp.broadcast_to(norms[0] + norms[1], (8, CHUNK))
        out_ref[:TOK] = jnp.maximum(preact, 0.0).astype(BF16)
        out_ref[TOK:] = stack_rows(pieces(norms[0], 3) + pieces(norms[1], 3))

    return call(
        body, "own_features", (mine, other, *parts, *squares, latent_bias), [IN_VMEM] * 8,
        [((ROWS, CHUNK), BF16), ((8, CHUNK), F32)], moved=16 * TOK * CHUNK,
    )


def rebuild_first(chunks, dec_t, own_weights):
    def body(*refs):
        feats, (dec_ref, weight_ref, out_ref) = refs[:FIRST_REBUILD], refs[FIRST_REBUILD:]
        acc = jnp.zeros((TOK, COL), F32)
        for feat, chunk in zip(feats, gathered_owners()):
            acc += dot(feat[:TOK], dec_ref[:, columns(chunk)], ((1,), (1,)))
        penalty = jnp.sum(feats[0][:TOK].astype(F32) * weight_ref[:1], axis=1, keepdims=True)
        out_ref[:, :COL] = acc
        out_ref[:, COL:] = jnp.broadcast_to(penalty, (TOK, WIDE - COL))

    return call(
        body, "rebuild_first", (*chunks, dec_t, own_weights), [IN_VMEM] * (FIRST_REBUILD + 2), [((TOK, WIDE), F32)],
        flops=2 * TOK * COL * CHUNK * FIRST_REBUILD, moved=2 * COL * LAT + 2 * TOK * LAT,
    )[0]


def rebuild_last(chunks, dec_t, partial):
    def body(*refs):
        feats, (dec_ref, partial_ref, out_ref) = refs[:8 - FIRST_REBUILD], refs[8 - FIRST_REBUILD:]
        acc = partial_ref[:, :COL]
        for feat, chunk in zip(feats, gathered_owners()[FIRST_REBUILD:]):
            acc += dot(feat[:TOK], dec_ref[:, columns(chunk)], ((1,), (1,)))
        out_ref[:, :COL] = acc.astype(BF16)
        out_ref[:, COL:] = partial_ref[:, COL:].astype(BF16)

    return call(
        body, "rebuild_last", (*chunks, dec_t, partial), [IN_VMEM] * (10 - FIRST_REBUILD), [((TOK, WIDE), BF16)],
        flops=2 * TOK * COL * CHUNK * (8 - FIRST_REBUILD), moved=2 * COL * LAT + 2 * TOK * LAT,
    )[0]


def offset_rows(act_t, output_bias):
    def body(act_ref, bias_ref, out_ref):
        first = lax.axis_index("latent") * 8
        token = lax.broadcasted_iota(jnp.int32, (8, TOK), 1)
        wanted = lax.broadcasted_iota(jnp.int32, (8, TOK), 0) + first
        pick = jnp.where(token == wanted, 1.0, 0.0).astype(BF16)
        out_ref[...] = bias_ref[...] - dot(pick, act_ref[...], ((1,), (1,)))

    return call(body, "offset_rows", (act_t, output_bias), [IN_VMEM] * 2, [((8, COL), F32)], moved=2 * TOK * COL)[0]


def error_rows(parts, offset):
    def body(parts_ref, offset_ref, out_ref):
        total = jnp.sum(parts_ref[...].astype(F32), axis=0)
        errors = total[:, :COL] + offset_ref[...]
        loss = 0.5 * jnp.sum(errors * errors, axis=1, keepdims=True) + SPARSITY * total[:, COL:COL + 1]
        lane = lax.broadcasted_iota(jnp.int32, (8, WIDE - COL), 1)
        tail = jnp.zeros((8, WIDE - COL), F32)
        for k, piece in enumerate(pieces(loss, 3)):
            tail = jnp.where(lane == k, piece, tail)
        out_ref[:, :, :COL] = jnp.broadcast_to(errors.astype(BF16)[None], (32, 8, COL))
        out_ref[:, :, COL:] = jnp.broadcast_to(tail.astype(BF16)[None], (32, 8, WIDE - COL))

    return call(
        body, "error_rows", (parts, offset), [IN_VMEM] * 2, [((32, 8, WIDE), BF16)], moved=4 * TOK * WIDE
    )[0]


def own_gradient(mine, other, parts, features, weights, errors):
    def body(mine_ref, other_ref, one_ref, two_ref, three_ref, feat_ref, weight_ref, tail_ref, out_ref):
        total = mine_ref[rows_of(0)] + other_ref[rows_of(0)].astype(F32)
        for ref in (one_ref, two_ref, three_ref):
            total += ref[...].astype(F32)
        total += SPARSITY * weight_ref[:1]
        out_ref[:TOK] = jnp.where(feat_ref[:TOK].astype(F32) > 0, total, 0.0).astype(BF16)
        loss = jnp.sum(jnp.sum(tail_ref[:, COL:].astype(F32), axis=0, keepdims=True), axis=1, keepdims=True)
        out_ref[TOK:] = stack_rows([jnp.broadcast_to(piece, (1, CHUNK)) for piece in pieces(loss, 3)])

    return call(
        body, "own_gradient", (mine, other, *parts, features, weights, errors), [IN_VMEM] * 8,
        [((ROWS, CHUNK), BF16)], moved=16 * TOK * CHUNK,
    )[0]


def store_chunks(values, owners, out_ref, buffer, sems):
    copies = []
    for k, chunk in enumerate(owners):
        buffer[k] = values(k, chunk)
        copies.append(pltpu.make_async_copy(buffer.at[k], out_ref.at[:, columns(chunk)], sems.at[k]))
        copies[-1].start()
    for copy in copies:
        copy.wait()


def decoder_gradient(errors, chunks, dec_t):
    def body(errors_ref, *refs):
        feats, (dec_ref, out_ref, sum_ref, buffer, sems) = refs[:8], refs[8:]
        x, _ = place()
        layer = x // 2
        error = errors_ref[:, :COL].T

        def values(k, chunk):
            feat = feats[k][:TOK]
            rows = feats[k][TOK:].astype(F32)
            norm = jnp.where(layer == 0, rows[0:1] + rows[1:2] + rows[2:3], rows[3:4] + rows[4:5] + rows[5:6])
            totals = jnp.sum(feat.astype(F32), axis=0, keepdims=True)
            scale = SPARSITY * totals / norm
            return (dot(error, feat, ((1,), (0,))) + scale * dec_ref[:, columns(chunk)].astype(F32)).astype(BF16)

        store_chunks(values, gathered_owners(), out_ref, buffer, sems)
        sum_ref[...] = jnp.sum(errors_ref[:, :COL].astype(F32), axis=0, keepdims=True)

    return call(
        body, "decoder_gradient", (errors, *chunks, dec_t), [IN_VMEM] * 10,
        [((COL, LAT), BF16), ((1, COL), F32)], out_specs=[ANYWHERE, IN_VMEM],
        scratch=[pltpu.VMEM((8, COL, CHUNK), BF16), pltpu.SemaphoreType.DMA((8,))],
        flops=2 * TOK * COL * LAT, moved=4 * COL * LAT + 2 * TOK * LAT,
    )


def loss_rows(grads):
    loss = jnp.zeros((1, 128), F32)
    for grad in grads:
        rows = grad[TOK:, :128].astype(F32)
        loss += rows[0:1] + rows[1:2] + rows[2:3]
    return loss * (1.0 / (TOK * LAYERS * D))


def encoder_gradient(act_t, chunks):
    def body(act_ref, *refs):
        grads, (out_ref, sum_ref, loss_ref, buffer, sum_buf, loss_buf, sems, small_sems) = refs[:8], refs[8:]
        loss_buf[...] = loss_rows(grads)
        for grad, chunk in zip(grads, gathered_owners(BACKWARD)):
            sum_buf[:, columns(chunk)] = jnp.sum(grad[:TOK].astype(F32), axis=0, keepdims=True)
        small = [
            pltpu.make_async_copy(sum_buf, sum_ref, small_sems.at[0]),
            pltpu.make_async_copy(loss_buf, loss_ref, small_sems.at[1]),
        ]
        for copy in small:
            copy.start()
        store_chunks(
            lambda k, chunk: dot(act_ref[...], grads[k][:TOK], ((1,), (0,))).astype(BF16),
            gathered_owners(BACKWARD), out_ref, buffer, sems,
        )
        for copy in small:
            copy.wait()

    return call(
        body, "encoder_gradient", (act_t, *chunks), [IN_VMEM] * 9,
        [((COL, LAT), BF16), ((1, LAT), F32), ((1, 128), F32)], out_specs=[ANYWHERE] * 3,
        scratch=[
            pltpu.VMEM((8, COL, CHUNK), BF16), pltpu.VMEM((1, LAT), F32), pltpu.VMEM((1, 128), F32),
            pltpu.SemaphoreType.DMA((8,)), pltpu.SemaphoreType.DMA((2,)),
        ],
        flops=2 * TOK * COL * LAT, moved=2 * COL * LAT + 2 * TOK * LAT,
    )


def gather_chunks(own, hops):
    moved = [own] + [on_width(own, x_shift(d)) for d in hops]
    return [chunk for part in moved for chunk in (part, on_width(part, CORE_SWAP))]


def shards(activations, encoder, latent_bias, decoder, output_bias):
    act_t, dec_t = activations.T, decoder.T

    send, keep_far, act, enc = preact_far(act_t, encoder)
    send, early_dec = lax.optimization_barrier((send, dec_t))
    squares = square_sums(early_dec)
    squares = (squares, on_width(squares, CORE_SWAP))
    far = (keep_far, on_width(send, CORE_SWAP))
    send = rest_parts(act, enc, True, F32, "preact_send")
    keep = rest_parts(act, enc, False, F32, "preact_keep")
    coded, send, keep = lax.optimization_barrier((encode(*far, squares, FAR), send, keep))
    rest = (keep, on_width(send, CORE_SWAP))
    coded = [on_width(coded, x_shift(FAR))] + [on_width(encode(*rest, squares, d), x_shift(d)) for d in HOPS[1:]]
    features, own_weights = own_features(*rest, coded, squares, latent_bias[None, :])

    feature_chunks = gather_chunks(features, FORWARD)
    partial = rebuild_first(feature_chunks[:FIRST_REBUILD], dec_t, own_weights)
    parts = rebuild_last(feature_chunks[FIRST_REBUILD:], dec_t, partial).reshape(32, 8, WIDE)
    parts, offset = lax.optimization_barrier((parts, offset_rows(act_t, output_bias[None, :])))
    parts = lax.all_to_all(parts, "latent", 0, 0)
    errors = error_rows(parts, offset)
    errors = lax.all_to_all(errors, "latent", 0, 0).reshape(TOK, WIDE)

    send = back_far(errors, dec_t)
    send, errors = lax.optimization_barrier((send, errors))
    keep_far, keep = back_keep(errors, dec_t)
    summed = keep_far + on_width(send, CORE_SWAP).astype(F32)
    send = rest_parts(errors, dec_t, True, BF16, "back_send")
    summed, keep = lax.optimization_barrier((summed.astype(BF16), keep))
    summed = [on_width(summed, x_shift(FAR))]
    rest = (keep, on_width(send, CORE_SWAP))
    for d in HOPS[1:]:
        total = rest[0][rows_of(d)] + rest[1][rows_of(d)].astype(F32)
        summed.append(on_width(total.astype(BF16), x_shift(d)))
    decoder_grad, output_grad = decoder_gradient(errors, feature_chunks, dec_t)
    decoder_grad, output_grad, features = lax.optimization_barrier((decoder_grad, output_grad[0], features))
    grad_pre = own_gradient(*rest, summed, features, own_weights, errors)
    encoder_grad, latent_grad, loss_value = encoder_gradient(act_t, gather_chunks(grad_pre, BACKWARD))
    return (loss_value[0, 0], encoder_grad, latent_grad[0], decoder_grad.T, output_grad)


def solution(mesh):
    placed = (P(None, "width"), P("width", "latent"), P("latent"), P("latent", "width"), P("width"))
    return jax.shard_map(
        shards,
        mesh=mesh,
        in_specs=placed,
        out_specs=(P(), P("width", "latent"), P("latent"), P("latent", "width"), P("width")),
        check_vma=False,
    )
```
